256 devices in a mesh: expert: 64 (over z, y, core), dp: 4 (over x).
Axes of the slice: x: 4, y: 4, z: 8, core: 2. Of those that a mesh axis runs over, the one named last changes fastest.
Arguments:
- tokens: bfloat16 [32768, 4096], P(('expert', 'dp')), may hold values from -700 to 700
- norm_gain: bfloat16 [4096], replicated, may hold values from 0.099609375 to 1.8984375
- route_ids: int32 [32768, 4], P(('expert', 'dp')), may hold values from 0 to 63, all different within a row; in each aligned block of 128 rows (0 to 127, 128 to 255, ...) at most 10 rows name the same one
- route_weights: bfloat16 [32768, 4], P(('expert', 'dp')), may hold values from 0.049804688 to 1
- gate_q: bfloat16 [64, 4096, 768], P('expert', 'dp'), may hold values from -0.09375 to 0.09375
- gate_scale: bfloat16 [64, 32, 6], P('expert', 'dp'), may hold values from 0.5 to 2, as said below
- up_q: bfloat16 [64, 4096, 768], P('expert', 'dp'), may hold values from -0.09375 to 0.09375
- up_scale: bfloat16 [64, 32, 6], P('expert', 'dp'), may hold values from 0.5 to 2, as said below
- down_q: bfloat16 [64, 768, 4096], P('expert', None, 'dp'), may hold values from -0.21875 to 0.21875
- down_scale: bfloat16 [64, 6, 32], P('expert', None, 'dp'), may hold values from 0.5 to 2, as said below
Outputs:
- moe_out: bfloat16 [32768, 4096], P(('expert', 'dp'))
The draws below stay inside these ranges and needn't reach their ends.
Inputs may be any that keep to these rules, and one draw needn't show every extreme that they name: `route_ids`: in the rows of one device (aligned blocks of 128 rows) no expert is named by more than 10 rows, a bound that some block reaches; the ids of one row differ. `gate_scale`: every entry is 0.5, 1 or 2. `up_scale`: every entry is 0.5, 1 or 2. `down_scale`: every entry is 0.5, 1 or 2.
All inputs are finite; a program needn't handle non-finite values.
Results may differ from the reference program's by a relative error of at most 0.0071.
Values may be sent and summed in bfloat16 or wider, within the bound.
No kernel may reach another device: no remote copies, remote signals or barrier semaphores. Data moves between devices by JAX's collectives and lax.ppermute only.
A program may use at most 192 MiB of HBM per device.

```python
import math
import jax
import jax.numpy as jnp
import numpy as np
from jax import lax

D = 4096
FFW = 768
TOP = 4
QB = 128
TOK_DEV = 128
EXPERTS = 64
TOKENS = 32768
CAP = 10


def draw_tokens(key, part):
    row_key, col_key, base_key = jax.random.split(key, 3)
    row_scale = jnp.exp(jax.random.uniform(row_key, (TOKENS, 1), jnp.float32, 0.0, math.log(10.0)))
    col_scale = jnp.exp(jax.random.uniform(col_key, (1, D), jnp.float32, 0.0, math.log(10.0)))
    base = jax.random.truncated_normal(base_key, -6.0, 6.0, (TOKENS, D), jnp.float32)
    return (base * row_scale * col_scale).astype(jnp.bfloat16)


def power_scales(key, shape):
    levels = jax.random.randint(key, shape, 0, 3)
    table = jnp.array([0.5, 1.0, 2.0], jnp.float32)
    return table[levels].astype(jnp.bfloat16)


def draw_gate_scale(key, part):
    return power_scales(jax.random.fold_in(key, 11), (EXPERTS, D // QB, FFW // QB))


def draw_up_scale(key, part):
    return power_scales(jax.random.fold_in(key, 23), (EXPERTS, D // QB, FFW // QB))


def draw_down_scale(key, part):
    return power_scales(jax.random.fold_in(key, 37), (EXPERTS, FFW // QB, D // QB))


def shard_levels(stream_key, shape, pieces, smallest, largest):
    level, own = 1.0, jax.random.fold_in(stream_key, 6)
    for axis_at, parts in pieces:
        steps = jnp.exp(jax.random.uniform(jax.random.fold_in(own, axis_at), (parts,), jnp.float32, smallest / len(pieces), largest / len(pieces)))
        level = level * jnp.repeat(steps, shape[axis_at] // parts).reshape([-1 if axis == axis_at else 1 for axis in range(len(shape))])
    return level


def routed_block(key, own, number, rows, amount, top, most, lean):
    order = jax.random.permutation(key, amount)
    heavy_load, common = load_shares(amount, rows * top, most, lean, True), load_shares(amount, rows * top, most, lean, False)
    places = jnp.arange(amount)

    def named(sizes, offset_by):
        used = int((sizes > 0).sum())
        fixed = max(1, used // 4)
        shifted = fixed + (places - fixed + offset_by * (used - fixed)) % max(1, amount - fixed)
        return jnp.zeros((amount,), jnp.int32).at[order[jnp.where(places < fixed, places, shifted)]].set(jnp.asarray(sizes, jnp.int32))

    sizes = jnp.where(number % 4 == 0, named(heavy_load, number // 4), named(common, number - number // 4 - 1))
    mixed = jax.random.permutation(jax.random.fold_in(own, 3), amount)
    giver, receiver = mixed[0:amount // 2 * 2:2], mixed[1:amount // 2 * 2:2]
    slack = jnp.minimum(sizes[giver] - 1, most - sizes[receiver]) // 2
    slack = jnp.where((giver == order[0]) | (receiver == order[0]) | (sizes[receiver] == 0), 0, jnp.maximum(slack, 0))
    shifted = jax.random.randint(jax.random.fold_in(own, 4), (amount // 2,), 0, 1 << 20) % (slack + 1)
    sizes = sizes.at[giver].add(-shifted).at[receiver].add(shifted)
    labels = jnp.searchsorted(jnp.cumsum(sizes), jnp.arange(rows * top), side="right").astype(jnp.int32)
    grid = labels.reshape(top, rows).T
    grid = grid[jax.random.permutation(jax.random.fold_in(own, 1), rows)]
    offset_by = jax.random.randint(jax.random.fold_in(own, 2), (rows, 1), 0, top)
    return jnp.take_along_axis(grid, (jnp.arange(top)[None, :] + offset_by) % top, axis=1)


def load_shares(number_of, total, most, skew, full):
    loads = [(1 << 20) // math.isqrt(grade ** skew) + 1 for grade in range(1, number_of + 1)]
    largest = most if full else min(most, max(-(-total // number_of), total * loads[0] // sum(loads)))
    least = 1 if total - largest >= number_of - 1 else 0
    counts, spare = [largest] + [least] * (number_of - 1), total - largest - least * (number_of - 1)
    while spare > 0:
        movable = [i for i in range(1, number_of) if counts[i] < largest] or [i for i in range(1, number_of) if counts[i] < most]
        whole, remaining = sum([loads[i] for i in movable]), spare
        for i in movable:
            extra = min(most - counts[i], max(1, remaining * loads[i] // whole), spare)
            counts[i] = counts[i] + extra
            spare = spare - extra
    return np.array(counts)


def scatter_about(stream_key, dims, width, limit, cuts=(), held_as=jnp.bfloat16):
    values = width * jax.random.normal(stream_key, dims, jnp.float32)
    if cuts:
        values = values * shard_levels(stream_key, dims, cuts, -0.22, 0.18)
    return jnp.clip(values, -limit, limit).astype(held_as)


def setup_inputs(seed: int = 0) -> dict:
    key_list = jax.random.split(jax.random.key(seed), 11)
    tokens = draw_tokens(jax.random.fold_in(key_list[10], 71), 0)
    norm_gain = jnp.clip(1.0 + 0.18 * jax.random.normal(key_list[1], (D,), jnp.float32), 0.099609375, 1.8984375).astype(jnp.bfloat16)
    route_ids_keys = jax.random.split(jax.random.fold_in(key_list[2], 1), TOKENS // TOK_DEV)
    route_ids_turns = jax.random.permutation(jax.random.fold_in(key_list[2], 3), TOKENS // TOK_DEV)
    route_ids = jax.vmap(lambda own, number: routed_block(jax.random.fold_in(key_list[2], 2), own, number, TOK_DEV, EXPERTS, TOP, CAP, 2))(route_ids_keys, route_ids_turns).reshape((TOKENS, TOP))
    route_weights = jnp.clip(jnp.exp(math.log(1.0) - 2.9996462 * jax.random.uniform(key_list[3], (TOKENS, TOP), jnp.float32) ** shard_levels(key_list[3], (TOKENS, TOP), ((0, 256),), -0.2, 0.2)), 0.049804688, 1.0).astype(jnp.bfloat16)
    gate_q = scatter_about(key_list[4], (EXPERTS, D, FFW), D ** -0.5, 0.09375, ((0, 64), (1, 4)))
    gate_scale = draw_gate_scale(jax.random.fold_in(key_list[10], 71), 0)
    up_q = scatter_about(key_list[6], (EXPERTS, D, FFW), D ** -0.5, 0.09375, ((0, 64), (1, 4)))
    up_scale = draw_up_scale(jax.random.fold_in(key_list[10], 71), 0)
    down_q = scatter_about(key_list[8], (EXPERTS, FFW, D), FFW ** -0.5, 0.21875, ((0, 64), (2, 4)))
    down_scale = draw_down_scale(jax.random.fold_in(key_list[10], 71), 0)
    return dict(tokens=tokens, norm_gain=norm_gain, route_ids=route_ids, route_weights=route_weights, gate_q=gate_q, gate_scale=gate_scale, up_q=up_q, up_scale=up_scale, down_q=down_q, down_scale=down_scale)


def expand_blocks(quantized, scales):
    block_size = quantized.shape[0] // scales.shape[0]
    widened = jnp.repeat(jnp.repeat(scales, block_size, axis=0), block_size, axis=1)
    return quantized * widened

def reference(tokens, norm_gain, route_ids, route_weights, gate_q, gate_scale, up_q, up_scale, down_q, down_scale):
    values = tokens.astype(jnp.float32)
    mean_square = lax.optimization_barrier(jnp.mean(values * values, axis=-1, keepdims=True))
    normed = (values * lax.rsqrt(mean_square + 1e-06) * norm_gain.astype(jnp.float32)).astype(jnp.bfloat16)
    flat_ids = route_ids.reshape(-1).astype(jnp.int32)
    flat_weights = route_weights.reshape(-1).astype(jnp.float32)
    row_limit = TOKENS // TOK_DEV * CAP

    def visit_expert(summed, expert):
        matches = flat_ids == expert
        chosen = jnp.nonzero(matches, size=row_limit, fill_value=0)[0].astype(jnp.int32)
        live_count = jnp.sum(matches.astype(jnp.int32))
        is_live = (jnp.arange(row_limit, dtype=jnp.int32) < live_count).astype(jnp.float32)
        owner_token = chosen // TOP
        expert_rows = normed[owner_token]
        gate_pre = jnp.dot(expert_rows, expand_blocks(gate_q[expert], gate_scale[expert]), preferred_element_type=jnp.float32)
        up_pre = jnp.dot(expert_rows, expand_blocks(up_q[expert], up_scale[expert]), preferred_element_type=jnp.float32)
        hidden = (jax.nn.silu(gate_pre) * up_pre).astype(jnp.bfloat16)
        expert_out = jnp.dot(hidden, expand_blocks(down_q[expert], down_scale[expert]), preferred_element_type=jnp.float32)
        shares = (expert_out * flat_weights[chosen][:, None]).astype(jnp.bfloat16)
        shares = lax.optimization_barrier(shares).astype(jnp.float32) * is_live[:, None]
        return (summed.at[owner_token].add(shares), None)
    summed, _ = lax.scan(visit_expert, jnp.zeros((TOKENS, D), jnp.float32), jnp.arange(EXPERTS, dtype=jnp.int32))
    return summed.astype(jnp.bfloat16)
```

```python
import functools

import jax
import jax.numpy as jnp
from jax import lax
from jax.experimental import pallas as pl
from jax.experimental.pallas import tpu as pltpu
from jax.sharding import Mesh
from jax.sharding import PartitionSpec as P

BF = jnp.bfloat16
F32 = jnp.float32
VMEM_LIMIT = 52 * 1024 * 1024
CAP = 10
NZ, NY, NC, NX = 8, 4, 2, 4
GROUPS = ((0, -1, 1, -2), (2, -3, 3, 4))


def params(**kw):
    return pltpu.CompilerParams(vmem_limit_bytes=VMEM_LIMIT, **kw)


def shift(array, axis, size, by):
    return lax.ppermute(array, axis, [(i, (i + by) % size) for i in range(size)])


def shift_plane(array, dy, dc):
    pairs = [
        (y * NC + c, ((y + dy) % NY) * NC + (c + dc) % NC) for y in range(NY) for c in range(NC)
    ]
    return lax.ppermute(array, ("y", "core"), pairs)


def norm_kernel(tok_ref, gain_ref, out_ref):
    values = tok_ref[...].astype(F32)
    mean_square = jnp.mean(values * values, axis=-1, keepdims=True)
    out_ref[...] = (values * lax.rsqrt(mean_square + 1e-06) * gain_ref[...].astype(F32)).astype(BF)


def rms_rows(tokens, gain):
    rows, width = tokens.shape
    tile = 32
    return pl.pallas_call(
        norm_kernel,
        grid=(rows // tile,),
        in_specs=[
            pl.BlockSpec((tile, width), lambda i: (i, 0)),
            pl.BlockSpec((1, width), lambda i: (0, 0)),
        ],
        out_specs=pl.BlockSpec((tile, width), lambda i: (i, 0)),
        out_shape=jax.ShapeDtypeStruct((rows, width), BF),
        compiler_params=params(),
        name="rms_rows",
    )(tokens, gain.reshape(1, width))


def scale_kernel(scale_ref, q_ref, out_ref):
    rows, cols = q_ref.shape
    i = pl.program_id(0)
    for c in range(cols // 128):
        s = scale_ref[i, c]
        out_ref[:, c * 128 : (c + 1) * 128] = (
            q_ref[:, c * 128 : (c + 1) * 128].astype(F32) * s
        ).astype(BF)


def scaled(quantized, scales):
    rows, cols = quantized.shape
    return pl.pallas_call(
        scale_kernel,
        grid=(rows // 128,),
        in_specs=[
            pl.BlockSpec(memory_space=pltpu.SMEM),
            pl.BlockSpec((128, cols), lambda i: (i, 0)),
        ],
        out_specs=pl.BlockSpec((128, cols), lambda i: (i, 0)),
        out_shape=jax.ShapeDtypeStruct((rows, cols), BF),
        compiler_params=params(),
        name="scaled",
    )(scales.astype(F32), quantized)


def dispatch_kernel(count, blocks, sel_ref, *refs):
    chunks, outs = refs[:count], refs[count:]
    at, total = 0, None
    for ref in chunks:
        rows = ref.shape[0]
        part = jnp.dot(sel_ref[:, at : at + rows], ref[...], preferred_element_type=F32)
        total = part if total is None else total + part
        at += rows
    block = outs[0].shape[0]
    for b in range(blocks):
        outs[b][...] = total[b * block : (b + 1) * block].astype(BF)


def dispatch(select, chunks):
    blocks = NY * NC
    block = select.shape[0] // blocks
    width = chunks[0].shape[1]
    tile = min(1024, width)
    return pl.pallas_call(
        functools.partial(dispatch_kernel, len(chunks), blocks),
        grid=(width // tile,),
        in_specs=[pl.BlockSpec(select.shape, lambda i: (0, 0))]
        + [pl.BlockSpec((c.shape[0], tile), lambda i: (0, i)) for c in chunks],
        out_specs=[pl.BlockSpec((block, tile), lambda i: (0, i))] * blocks,
        out_shape=[jax.ShapeDtypeStruct((block, width), BF)] * blocks,
        compiler_params=params(),
        name="dispatch",
    )(select, *chunks)


def hidden_kernel(x_at, rows_ref, *refs):
    gates, ups, out_ref = refs[:5], refs[5:10], refs[10]
    depth = gates[0].shape[0]
    own = x_at[0]

    def project(pieces):
        total = None
        for n, ref in enumerate(pieces):
            place = lax.rem(own + (0, NX - 1, 1, 2, 2)[n], NX) * depth
            if n == 4:
                place = place + ref.shape[0]
            cols = pl.ds(pl.multiple_of(place, 128), ref.shape[0])
            part = jnp.dot(rows_ref[:, cols], ref[...], preferred_element_type=F32)
            total = part if total is None else total + part
        return total

    gate = project(gates)
    up = project(ups)
    out_ref[...] = (gate / (1.0 + jnp.exp(-gate)) * up).astype(BF)


def hidden_units(x_at, rows, gates, ups):
    count, width = rows.shape
    units = gates[0].shape[1]
    tile = 256
    return pl.pallas_call(
        hidden_kernel,
        grid_spec=pltpu.PrefetchScalarGridSpec(
            num_scalar_prefetch=1,
            grid=(units // tile,),
            in_specs=[pl.BlockSpec((count, width), lambda i, s: (0, 0))]
            + [pl.BlockSpec((w.shape[0], tile), lambda i, s: (0, i)) for w in (*gates, *ups)],
            out_specs=pl.BlockSpec((count, tile), lambda i, s: (0, i)),
        ),
        out_shape=jax.ShapeDtypeStruct((count, units), BF),
        compiler_params=params(),
        name="hidden_units",
    )(x_at, rows, *gates, *ups)


def down_kernel(pieces, hidden_ref, *refs):
    weights, outs = refs[:pieces], refs[pieces:]
    at, total = 0, None
    for ref in weights:
        rows = ref.shape[0]
        part = jnp.dot(hidden_ref[:, at : at + rows], ref[...], preferred_element_type=F32)
        total = part if total is None else total + part
        at += rows
    block = outs[0].shape[0]
    for b, out in enumerate(outs):
        out[...] = total[b * block : (b + 1) * block].astype(BF)


def project_down(hidden, weights):
    blocks = NY * NC
    block = hidden.shape[0] // blocks
    width = weights[0].shape[1]
    tile = min(512, width)
    return pl.pallas_call(
        functools.partial(down_kernel, len(weights)),
        grid=(width // tile,),
        in_specs=[pl.BlockSpec(hidden.shape, lambda i: (0, 0))]
        + [pl.BlockSpec((w.shape[0], tile), lambda i: (0, i)) for w in weights],
        out_specs=[pl.BlockSpec((block, tile), lambda i: (0, i))] * blocks,
        out_shape=[jax.ShapeDtypeStruct((block, width), BF)] * blocks,
        compiler_params=params(),
        name="project_down",
    )(hidden, *weights)


def combine_kernel(blocks, sizes, mix_ref, *refs):
    parts, outs, rows_ref = refs[:blocks], refs[blocks:-1], refs[-1]
    block = parts[0].shape[0]
    for b in range(blocks):
        rows_ref[b * block : (b + 1) * block, :] = parts[b][...]
    at = 0
    for size, out in zip(sizes, outs):
        out[...] = jnp.dot(
            mix_ref[at : at + size, :], rows_ref[...], preferred_element_type=F32
        ).astype(BF)
        at += size


def combine(mix, parts, sizes):
    width = parts[0].shape[1]
    tile = min(512, width)
    block = parts[0].shape[0]
    return pl.pallas_call(
        functools.partial(combine_kernel, len(parts), sizes),
        grid=(width // tile,),
        in_specs=[pl.BlockSpec(mix.shape, lambda i: (0, 0))]
        + [pl.BlockSpec((block, tile), lambda i: (0, i))] * len(parts),
        out_specs=[pl.BlockSpec((size, tile), lambda i: (0, i)) for size in sizes],
        out_shape=[jax.ShapeDtypeStruct((size, width), BF) for size in sizes],
        scratch_shapes=[pltpu.VMEM((block * len(parts), tile), BF)],
        compiler_params=params(),
        name="combine",
    )(mix, *parts)


def finish_kernel(x_at, *refs):
    parts, out_ref = refs[:-1], refs[-1]
    width = parts[0].shape[1]
    own = x_at[0]
    for n, offset in enumerate((0, NX - 1, 1, 2)):
        kept, forward, backward = parts[3 * n : 3 * n + 3]
        total = kept[...].astype(F32) + forward[...].astype(F32) + backward[...].astype(F32)
        place = pl.multiple_of(lax.rem(own + offset, NX) * width, 128)
        out_ref[:, pl.ds(place, width)] = total.astype(BF)


def finish(x_at, parts):
    rows, width = parts[0].shape
    return pl.pallas_call(
        finish_kernel,
        grid_spec=pltpu.PrefetchScalarGridSpec(
            num_scalar_prefetch=1,
            grid=(1,),
            in_specs=[pl.BlockSpec((rows, width), lambda i, s: (0, 0))] * len(parts),
            out_specs=pl.BlockSpec((rows, width * NX), lambda i, s: (0, 0)),
        ),
        out_shape=jax.ShapeDtypeStruct((rows, width * NX), BF),
        compiler_params=params(),
        name="finish",
    )(x_at, *parts)


def gather_over_x(piece):
    half = piece.shape[0] // 2
    low = shift(piece, "x", NX, 1)
    high = shift(piece, "x", NX, -1)
    far_top = shift(low[:half], "x", NX, 1)
    far_bottom = shift(high[half:], "x", NX, -1)
    return [piece, low, high, far_top, far_bottom]


def body(
    tokens,
    norm_gain,
    route_ids,
    route_weights,
    gate_q,
    gate_scale,
    up_q,
    up_scale,
    down_q,
    down_scale,
):
    tok_rows, model_width = tokens.shape
    top = route_ids.shape[1]
    experts = NZ * NY * NC
    plane = NY * NC
    half = tok_rows // 2
    z, y, c, x = (lax.axis_index(a) for a in ("z", "y", "core", "x"))
    x_at = jnp.reshape(x, (1,)).astype(jnp.int32)

    gates = gather_over_x(scaled(gate_q[0], gate_scale[0]))
    ups = gather_over_x(scaled(up_q[0], up_scale[0]))
    down_own = scaled(down_q[0], down_scale[0])
    down_own, _ = lax.optimization_barrier((down_own, ups[1]))
    downs = gather_over_x(down_own)

    normed = rms_rows(tokens, norm_gain)
    chunks = {0: [normed]}
    ahead = behind = normed
    for step in (1, 2, 3):
        ahead = shift(ahead, "z", NZ, 1)
        behind = shift(behind, "z", NZ, -1)
        chunks[-step], chunks[step] = [ahead], [behind]
    chunks[4] = [shift(ahead[:half], "z", NZ, 1), shift(behind[half:], "z", NZ, -1)]

    counts = jnp.sum(
        (route_ids[:, :, None] == jnp.arange(experts, dtype=jnp.int32)).astype(F32), axis=1
    )
    earlier = (
        jnp.arange(tok_rows)[:, None] > jnp.arange(tok_rows)[None, :]
    ).astype(F32)
    before = jnp.dot(earlier, counts)
    chosen = route_ids[:, :, None] == jnp.arange(experts, dtype=jnp.int32)
    rank = jnp.sum(jnp.where(chosen, before[:, None, :], 0.0), axis=2)
    routes = jnp.concatenate(
        [route_ids.astype(BF), rank.astype(BF), route_weights.astype(BF)], axis=1
    )
    routes = lax.all_gather(routes, "z", axis=0, tiled=False)
    routes = jnp.concatenate([routes, routes], axis=0)
    routes = lax.dynamic_slice_in_dim(routes, z, NZ, axis=0)
    ids = routes[:, :, :top].astype(jnp.int32)
    ranks = routes[:, :, top : 2 * top].astype(jnp.int32)
    weights = routes[:, :, 2 * top :].astype(F32)
    local = ids % plane
    target = ((local // NC - y) % NY) * NC + (local % NC - c) % NC
    here = ids // plane == z

    block_rows = [-(-CAP * len(g) // 8) * 8 for g in GROUPS]
    stride = sum(block_rows)

    received = []
    for n, group in enumerate(GROUPS):
        rows = block_rows[n]
        place = jnp.stack(
            [
                jnp.where(here[j % NZ], target[j % NZ] * rows + i * CAP + ranks[j % NZ], -1)
                for i, j in enumerate(group)
            ]
        ).reshape(len(group) * tok_rows, top)
        slots = jnp.arange(plane * rows, dtype=jnp.int32)[:, None]
        select = sum((place[None, :, k] == slots).astype(F32) for k in range(top)).astype(BF)
        blocks = dispatch(select, [a for j in group for a in chunks[j]])
        received.append(
            [
                b if t == 0 else shift_plane(b, t // NC, t % NC)
                for t, b in enumerate(blocks)
            ]
        )
    rows_in = jnp.concatenate(
        [received[n][t] for t in range(plane) for n in range(len(GROUPS))], axis=0
    )

    hidden = hidden_units(x_at, rows_in, gates, ups)

    order = (4, 3, -3, 2, -2, 1, -1, 0)
    mixes = []
    for j in order:
        n = next(n for n, g in enumerate(GROUPS) if j in g)
        start = sum(block_rows[:n]) + GROUPS[n].index(j) * CAP
        place = jnp.where(here[j % NZ], target[j % NZ] * stride + start + ranks[j % NZ], -1)
        slots = jnp.arange(plane * stride, dtype=jnp.int32)[None, :]
        mixes.append(
            sum(
                jnp.where(place[:, k, None] == slots, weights[j % NZ][:, k, None], 0.0)
                for k in range(top)
            )
        )
    mix = jnp.concatenate(mixes, axis=0).astype(BF)
    sizes = [half, half] + [tok_rows] * (NZ - 1)

    def widen(part, top_half):
        zero = jnp.zeros_like(part)
        return jnp.concatenate([part, zero] if top_half else [zero, part], axis=0)

    def add(a, b):
        return (a.astype(F32) + b.astype(F32)).astype(BF)

    finals = []
    for weights_down in ([downs[0]], [downs[1]], [downs[2]], downs[3:]):
        outs = project_down(hidden, weights_down)
        back = [
            b if t == 0 else shift_plane(b, -(t // NC), t % NC) for t, b in enumerate(outs)
        ]
        sums = combine(mix, back, sizes)
        ahead = shift(sums[0], "z", NZ, 1)
        behind = shift(sums[1], "z", NZ, -1)
        ahead = shift(add(sums[2], widen(ahead, True)), "z", NZ, 1)
        behind = shift(add(sums[3], widen(behind, False)), "z", NZ, -1)
        for step in (4, 6):
            ahead = shift(add(sums[step], ahead), "z", NZ, 1)
            behind = shift(add(sums[step + 1], behind), "z", NZ, -1)
        finals += [sums[8], ahead, behind]
    return finish(x_at, finals)


def solution(mesh):
    assert mesh.devices.shape == (NZ * NY * NC, NX)
    fine = Mesh(mesh.devices.reshape(NZ, NY, NC, NX), ("z", "y", "core", "x"))
    expert = ("z", "y", "core")
    every = ("z", "y", "core", "x")
    in_specs = (
        P(every, None),
        P(),
        P(every, None),
        P(every, None),
        P(expert, "x", None),
        P(expert, "x", None),
        P(expert, "x", None),
        P(expert, "x", None),
        P(expert, None, "x"),
        P(expert, None, "x"),
    )
    return jax.shard_map(
        body, mesh=fine, in_specs=in_specs, out_specs=P(every, None), check_vma=False
    )
```

```python
import functools

import jax
import jax.numpy as jnp
from jax import lax
from jax.experimental import pallas as pl
from jax.experimental.pallas import tpu as pltpu
from jax.sharding import Mesh
from jax.sharding import PartitionSpec as P

BF = jnp.bfloat16
F32 = jnp.float32
VMEM_LIMIT = 52 * 1024 * 1024
CAP = 10
TOK, TOP = 128, 4
LANES = 128
NZ, NY, NC, NX = 8, 4, 2, 4
GROUPS = ((0, -1, 1, -2, 2), (-3, 3, 4))


def params(**kw):
    return pltpu.CompilerParams(vmem_limit_bytes=VMEM_LIMIT, **kw)


def shift(array, axis, size, by):
    return lax.ppermute(array, axis, [(i, (i + by) % size) for i in range(size)])


def exchange(blocks):
    return lax.all_to_all(blocks, ("y", "core"), split_axis=0, concat_axis=0, tiled=True)


def after(arrays, earlier):
    return lax.optimization_barrier((tuple(arrays), tuple(earlier)))[0]


def prepare_kernel(tok_ref, gain_ref, ids_ref, weights_ref, out_ref):
    rows, width = tok_ref.shape
    top = ids_ref.shape[1]
    values = tok_ref[...].astype(F32)
    mean_square = jnp.mean(values * values, axis=-1, keepdims=True)
    out_ref[:, :width] = (
        values * lax.rsqrt(mean_square + 1e-06) * gain_ref[...].astype(F32)
    ).astype(BF)
    experts = lax.broadcasted_iota(jnp.int32, (rows, LANES), 1)
    chosen = [(ids_ref[:, k : k + 1] == experts).astype(F32) for k in range(top)]
    counts = sum(chosen).astype(BF)
    earlier = (
        lax.broadcasted_iota(jnp.int32, (rows, rows), 0)
        > lax.broadcasted_iota(jnp.int32, (rows, rows), 1)
    )
    before = jnp.dot(earlier.astype(F32).astype(BF), counts, preferred_element_type=F32)
    lane = lax.broadcasted_iota(jnp.int32, (rows, LANES), 1)
    routes = jnp.zeros((rows, LANES), F32)
    for k in range(top):
        rank = jnp.sum(chosen[k] * before, axis=1, keepdims=True)
        routes = jnp.where(lane == k, ids_ref[:, k : k + 1].astype(F32), routes)
        routes = jnp.where(lane == top + k, rank, routes)
        routes = jnp.where(lane == 2 * top + k, weights_ref[:, k : k + 1].astype(F32), routes)
    out_ref[:, width:] = routes.astype(BF)


def prepare(tokens, gain, ids, weights):
    rows, width = tokens.shape
    return pl.pallas_call(
        prepare_kernel,
        out_shape=jax.ShapeDtypeStruct((rows, width + LANES), BF),
        compiler_params=params(),
        name="prepare",
    )(tokens, gain.reshape(1, width), ids, weights)


def scale_kernel(first, *refs):
    count = (len(refs) - 1) // 2
    scales, values, out_ref = refs[:count], refs[count : 2 * count], refs[-1]
    block = pl.program_id(0) + first
    at = 0
    for scale_ref, q_ref in zip(scales, values):
        for c in range(q_ref.shape[1] // 128):
            out_ref[:, at : at + 128] = (
                q_ref[:, c * 128 : (c + 1) * 128].astype(F32) * scale_ref[block, c]
            ).astype(BF)
            at += 128


def scaled(pairs, first, steps):
    cols = pairs[0][0].shape[1]
    return pl.pallas_call(
        functools.partial(scale_kernel, first),
        grid=(steps,),
        in_specs=[pl.BlockSpec(memory_space=pltpu.SMEM)] * len(pairs)
        + [pl.BlockSpec((128, cols), lambda i: (i + first, 0))] * len(pairs),
        out_specs=pl.BlockSpec((128, cols * len(pairs)), lambda i: (i, 0)),
        out_shape=jax.ShapeDtypeStruct((steps * 128, cols * len(pairs)), BF),
        compiler_params=params(),
        name="scaled",
    )(*[s.astype(F32) for _, s in pairs], *[q for q, _ in pairs])


def dispatch_kernel(sizes, rows, stride, start, z_at, *refs):
    count = len(sizes)
    chunks, routes = refs[:count], refs[count : 2 * count]
    out_ref, mixes, pick_ref = refs[2 * count], refs[2 * count + 1 : -1], refs[-1]
    plane = NY * NC

    @pl.when(pl.program_id(0) == 0)
    def _():
        low = (z_at[0] * plane).astype(F32)
        at, member, filled = 0, 0, 0
        for n, size in enumerate(sizes):
            info = routes[n][...].astype(F32)
            pick = jnp.zeros((size, plane * rows), F32)
            mix = jnp.zeros((size, plane * stride), F32)
            slots = lax.broadcasted_iota(jnp.int32, pick.shape, 1).astype(F32)
            wide = lax.broadcasted_iota(jnp.int32, mix.shape, 1).astype(F32)
            for k in range(TOP):
                local = info[:, k : k + 1] - low
                rank = info[:, TOP + k : TOP + k + 1] + float(member * CAP)
                weight = info[:, 2 * TOP + k : 2 * TOP + k + 1]
                here = (local >= 0.0) & (local < float(plane))
                pick += jnp.where(jnp.where(here, local * rows + rank, -1.0) == slots, 1.0, 0.0)
                mix += jnp.where(
                    jnp.where(here, local * stride + start + rank, -1.0) == wide, weight, 0.0
                )
            pick_ref[at : at + size, :] = pick.astype(BF)
            mixes[n][...] = mix.astype(BF)
            at += size
            filled += size
            if filled == TOK:
                member, filled = member + 1, 0

    at, total = 0, None
    for ref in chunks:
        size = ref.shape[0]
        part = lax.dot_general(
            pick_ref[at : at + size, :],
            ref[...],
            (((0,), (0,)), ((), ())),
            preferred_element_type=F32,
        )
        total = part if total is None else total + part
        at += size
    out_ref[...] = total.astype(BF)


def dispatch(z_at, chunks, rows, stride, start):
    plane = NY * NC
    sizes = [c.shape[0] for c in chunks]
    width = chunks[0].shape[1] - LANES
    tile = min(1024, width)
    outs = pl.pallas_call(
        functools.partial(dispatch_kernel, sizes, rows, stride, float(start)),
        grid_spec=pltpu.PrefetchScalarGridSpec(
            num_scalar_prefetch=1,
            grid=(width // tile,),
            in_specs=[pl.BlockSpec((s, tile), lambda i, z: (0, i)) for s in sizes]
            + [pl.BlockSpec((s, LANES), lambda i, z: (0, width // LANES)) for s in sizes],
            out_specs=[pl.BlockSpec((plane * rows, tile), lambda i, z: (0, i))]
            + [pl.BlockSpec((s, plane * stride), lambda i, z: (0, 0)) for s in sizes],
            scratch_shapes=[pltpu.VMEM((sum(sizes), plane * rows), BF)],
        ),
        out_shape=[jax.ShapeDtypeStruct((plane * rows, width), BF)]
        + [jax.ShapeDtypeStruct((s, plane * stride), BF) for s in sizes],
        compiler_params=params(),
        name="dispatch",
    )(z_at, *chunks, *chunks)
    return outs[0].reshape(plane, rows, width), outs[1:]


def hidden_kernel(places, x_at, rows_ref, *refs):
    count = len(places)
    gates, ups, out_ref = refs[:count], refs[count : 2 * count], refs[-1]
    depth = rows_ref.shape[1] // NX
    own = x_at[0]

    def project(pieces):
        total = None
        for (offset, inside), ref in zip(places, pieces):
            place = lax.rem(own + offset, NX) * depth + inside
            cols = pl.ds(pl.multiple_of(place, 128), ref.shape[0])
            part = jnp.dot(rows_ref[:, cols], ref[...], preferred_element_type=F32)
            total = part if total is None else total + part
        return total

    gate = project(gates)
    up = project(ups)
    out_ref[...] = (gate / (1.0 + jnp.exp(-gate)) * up).astype(BF)


def hidden_units(x_at, rows, places, pieces):
    count, width = rows.shape
    units = pieces[0].shape[1] // 2
    tile = 256
    steps = units // tile
    return pl.pallas_call(
        functools.partial(hidden_kernel, places),
        grid_spec=pltpu.PrefetchScalarGridSpec(
            num_scalar_prefetch=1,
            grid=(steps,),
            in_specs=[pl.BlockSpec((count, width), lambda i, s: (0, 0))]
            + [pl.BlockSpec((w.shape[0], tile), lambda i, s: (0, i)) for w in pieces]
            + [pl.BlockSpec((w.shape[0], tile), lambda i, s: (0, i + steps)) for w in pieces],
            out_specs=pl.BlockSpec((count, tile), lambda i, s: (0, i)),
        ),
        out_shape=jax.ShapeDtypeStruct((count, units), BF),
        compiler_params=params(),
        name="hidden_units",
    )(x_at, rows, *pieces, *pieces)


def down_kernel(hidden_ref, *refs):
    weights, out_ref = refs[:-1], refs[-1]
    at, total = 0, None
    for ref in weights:
        rows = ref.shape[0]
        part = jnp.dot(hidden_ref[:, at : at + rows], ref[...], preferred_element_type=F32)
        total = part if total is None else total + part
        at += rows
    out_ref[...] = total.astype(BF)


def project_down(hidden, weights):
    count = hidden.shape[0]
    width = weights[0].shape[1]
    tile = min(512, width)
    return pl.pallas_call(
        down_kernel,
        grid=(width // tile,),
        in_specs=[pl.BlockSpec(hidden.shape, lambda i: (0, 0))]
        + [pl.BlockSpec((w.shape[0], tile), lambda i: (0, i)) for w in weights],
        out_specs=pl.BlockSpec((count, tile), lambda i: (0, i)),
        out_shape=jax.ShapeDtypeStruct((count, width), BF),
        compiler_params=params(),
        name="project_down",
    )(hidden, *weights)


def combine_kernel(rows_ref, *refs):
    count = len(refs) // 2
    for mix_ref, out_ref in zip(refs[:count], refs[count:]):
        out_ref[...] = jnp.dot(
            mix_ref[...], rows_ref[...], preferred_element_type=F32
        ).astype(BF)


def combine(rows, mixes):
    count, width = rows.shape
    tile = min(512, width)
    return pl.pallas_call(
        combine_kernel,
        grid=(width // tile,),
        in_specs=[pl.BlockSpec((count, tile), lambda i: (0, i))]
        + [pl.BlockSpec(m.shape, lambda i: (0, 0)) for m in mixes],
        out_specs=[pl.BlockSpec((m.shape[0], tile), lambda i: (0, i)) for m in mixes],
        out_shape=[jax.ShapeDtypeStruct((m.shape[0], width), BF) for m in mixes],
        compiler_params=params(),
        name="combine",
    )(rows, *mixes)


def finish_kernel(x_at, *refs):
    parts, out_ref = refs[:-1], refs[-1]
    width = parts[0].shape[1]
    own = x_at[0]
    for n, offset in enumerate((0, NX - 1, 1, 2)):
        kept, forward, backward = parts[3 * n : 3 * n + 3]
        total = kept[...].astype(F32) + forward[...].astype(F32) + backward[...].astype(F32)
        place = pl.multiple_of(lax.rem(own + offset, NX) * width, 128)
        out_ref[:, pl.ds(place, width)] = total.astype(BF)


def finish(x_at, parts):
    rows, width = parts[0].shape
    return pl.pallas_call(
        finish_kernel,
        grid_spec=pltpu.PrefetchScalarGridSpec(
            num_scalar_prefetch=1,
            grid=(1,),
            in_specs=[pl.BlockSpec((rows, width), lambda i, s: (0, 0))] * len(parts),
            out_specs=pl.BlockSpec((rows, width * NX), lambda i, s: (0, 0)),
        ),
        out_shape=jax.ShapeDtypeStruct((rows, width * NX), BF),
        compiler_params=params(),
        name="finish",
    )(x_at, *parts)


def body(
    tokens,
    norm_gain,
    route_ids,
    route_weights,
    gate_q,
    gate_scale,
    up_q,
    up_scale,
    down_q,
    down_scale,
):
    tok_rows, width = tokens.shape
    units = down_q.shape[1]
    assert tok_rows == TOK and route_ids.shape[1] == TOP
    half = tok_rows // 2
    plane = NY * NC
    z_at = jnp.reshape(lax.axis_index("z"), (1,)).astype(jnp.int32)
    x_at = jnp.reshape(lax.axis_index("x"), (1,)).astype(jnp.int32)

    both = [(gate_q[0], gate_scale[0]), (up_q[0], up_scale[0])]
    blocks = gate_scale.shape[1]
    cut = 3 * blocks // 8
    first = scaled(both, 0, cut)
    second = scaled(both, cut, cut)
    rest = scaled(both, 2 * cut, blocks - 2 * cut)
    (tokens,) = after((tokens,), (first, second))
    own = prepare(tokens, norm_gain, route_ids, route_weights)

    def z_step(ahead, behind):
        return shift(ahead, "z", NZ, 1), shift(behind, "z", NZ, -1)

    def x_step(up, down):
        return shift(up, "x", NX, 1), shift(down, "x", NX, -1)

    chunks = {0: [own]}
    ahead, behind = z_step(own, own)
    low_first, high_second = x_step(first, second)
    chunks[-1], chunks[1] = [ahead], [behind]
    ahead, behind, up, down = after((ahead, behind, second, first), (low_first, high_second))
    ahead, behind = z_step(ahead, behind)
    low_second, high_first = x_step(up, down)
    ahead, behind, up, down = after(
        (ahead, behind, low_first, high_second), (low_second, high_first)
    )
    chunks[-2], chunks[2] = [ahead], [behind]
    ahead, behind = z_step(ahead, behind)
    far_first, far_second = x_step(up, down)
    chunks[-3], chunks[3] = [ahead], [behind]
    ahead, behind, up, down = after(
        (ahead[:half], behind[half:], rest, rest), (far_first, far_second)
    )
    ahead, behind = z_step(ahead, behind)
    low_rest, high_rest = x_step(up, down)
    ahead, behind = after((ahead, behind), (low_rest, high_rest))
    chunks[4] = [ahead, behind]
    split = rest.shape[0] // 2
    far_rest = x_step(low_rest[:split], high_rest[split:])
    gate_up = [first, second, rest, low_first, low_second, low_rest]
    gate_up += [high_first, high_second, high_rest, far_first, far_second, *far_rest]
    sides = (0, cut * 128, 2 * cut * 128)
    places = tuple((o, i) for o in (0, NX - 1, 1, 2) for i in sides)
    places += ((2, 2 * cut * 128 + split),)
    depth = width // NX

    down_pair = [(down_q[0], down_scale[0])]
    down_own = scaled(down_pair, 0, units // 128)
    (down_own,) = after((down_own,), far_rest)
    low, high = x_step(down_own, down_own)
    low_top, high_bottom = low[: units // 2], high[units // 2 :]
    downs = [[down_own], [low], [high], x_step(low_top, high_bottom)]

    block_rows = [-(-CAP * len(g) // 8) * 8 for g in GROUPS]
    stride = CAP * NZ
    hidden, mixes, start = [], {}, 0
    for n, group in enumerate(GROUPS):
        arrays = [a for j in group for a in chunks[j]]
        blocks, weights = dispatch(z_at, arrays, block_rows[n], stride, start)
        weights = list(weights)
        for j in group:
            mixes[j] = [weights.pop(0) for _ in chunks[j]]
        rows_in = exchange(blocks).reshape(plane * block_rows[n], width)
        units_out = hidden_units(x_at, rows_in, places, gate_up)
        used = CAP * len(group)
        hidden.append(units_out.reshape(plane, block_rows[n], units)[:, :used])
        start += used
    hidden = jnp.concatenate(hidden, axis=1).reshape(plane * stride, units)

    order = [m for j in (4, 3, -3, 2, -2, 1, -1, 0) for m in mixes[j]]

    def add(a, b):
        return (a.astype(F32) + b.astype(F32)).astype(BF)

    def add_rows(a, b, at):
        return jnp.concatenate(
            [add(a[:half], b), a[half:]] if at == 0 else [a[:half], add(a[half:], b)], axis=0
        )

    finals, sums = [], ()
    for s in range(NX):
        (out,) = after((project_down(hidden, downs[s]),), sums)
        back = exchange(out.reshape(plane, stride, depth)).reshape(plane * stride, depth)
        sums = combine(back, order)
        ahead = shift(sums[0], "z", NZ, 1)
        behind = shift(sums[1], "z", NZ, -1)
        ahead = shift(add_rows(sums[2], ahead, 0), "z", NZ, 1)
        behind = shift(add_rows(sums[3], behind, half), "z", NZ, -1)
        for step in (4, 6):
            ahead = shift(add(sums[step], ahead), "z", NZ, 1)
            behind = shift(add(sums[step + 1], behind), "z", NZ, -1)
        finals += [sums[8], ahead, behind]
    return finish(x_at, finals)


def solution(mesh):
    assert mesh.devices.shape == (NZ * NY * NC, NX)
    fine = Mesh(mesh.devices.reshape(NZ, NY, NC, NX), ("z", "y", "core", "x"))
    expert = ("z", "y", "core")
    every = ("z", "y", "core", "x")
    in_specs = (
        P(every, None),
        P(),
        P(every, None),
        P(every, None),
        P(expert, "x", None),
        P(expert, "x", None),
        P(expert, "x", None),
        P(expert, "x", None),
        P(expert, None, "x"),
        P(expert, None, "x"),
    )
    return jax.shard_map(
        body, mesh=fine, in_specs=in_specs, out_specs=P(every, None), check_vma=False
    )
```

```python
import functools

import jax
import jax.numpy as jnp
from jax import lax
from jax.experimental import pallas as pl
from jax.experimental.pallas import tpu as pltpu
from jax.sharding import Mesh
from jax.sharding import PartitionSpec as P

BF = jnp.bfloat16
F32 = jnp.float32
VMEM_LIMIT = 52 * 1024 * 1024
CAP = 10
TOK, TOP = 128, 4
LANES = 128
SLICES = (("own", "low"), ("high", "far"))
HOLD = 4
DOWN_AFTER = 2
NZ, NY, NC, NX = 8, 4, 2, 4
GROUPS = (((0, -1, 1), (-2, 2)), ((-3, 3), (4,)))


def params(**kw):
    return pltpu.CompilerParams(vmem_limit_bytes=VMEM_LIMIT, **kw)


def shift(array, axis, size, by):
    return lax.ppermute(array, axis, [(i, (i + by) % size) for i in range(size)])


def exchange(blocks):
    return lax.all_to_all(blocks, ("y", "core"), split_axis=0, concat_axis=0, tiled=True)


def after(arrays, earlier):
    return lax.optimization_barrier((tuple(arrays), tuple(earlier)))[0]


def prepare_kernel(tok_ref, gain_ref, ids_ref, weights_ref, *outs):
    rows, width = tok_ref.shape
    half = rows // 2
    top = ids_ref.shape[1]
    experts = lax.broadcasted_iota(jnp.int32, (rows, LANES), 1)
    chosen = [(ids_ref[:, k : k + 1] == experts).astype(F32) for k in range(top)]
    counts = sum(chosen).astype(BF)
    earlier = (
        lax.broadcasted_iota(jnp.int32, (rows, rows), 0)
        > lax.broadcasted_iota(jnp.int32, (rows, rows), 1)
    )
    before = jnp.dot(earlier.astype(F32).astype(BF), counts, preferred_element_type=F32)
    lane = lax.broadcasted_iota(jnp.int32, (rows, LANES), 1)
    routes = jnp.zeros((rows, LANES), F32)
    for k in range(top):
        rank = jnp.sum(chosen[k] * before, axis=1, keepdims=True)
        routes = jnp.where(lane == k, ids_ref[:, k : k + 1].astype(F32), routes)
        routes = jnp.where(lane == top + k, rank, routes)
        routes = jnp.where(lane == 2 * top + k, weights_ref[:, k : k + 1].astype(F32), routes)
    routes = routes.astype(BF)
    for n, out_ref in enumerate(outs):
        values = tok_ref[n * half : (n + 1) * half, :].astype(F32)
        mean_square = jnp.mean(values * values, axis=-1, keepdims=True)
        out_ref[:, :width] = (
            values * lax.rsqrt(mean_square + 1e-06) * gain_ref[...].astype(F32)
        ).astype(BF)
        out_ref[:, width:] = routes[n * half : (n + 1) * half]


def prepare(tokens, gain, ids, weights):
    rows, width = tokens.shape
    half = jax.ShapeDtypeStruct((rows // 2, width + LANES), BF)
    return pl.pallas_call(
        prepare_kernel,
        out_shape=[half, half],
        compiler_params=params(),
        name="prepare",
    )(tokens, gain.reshape(1, width), ids, weights)


def scale_kernel(*refs):
    count = (len(refs) - 1) // 2
    scales, values, out_ref = refs[:count], refs[count : 2 * count], refs[-1]
    rows = values[0].shape[0]
    at = 0
    for scale_ref, q_ref in zip(scales, values):
        for c in range(q_ref.shape[1] // 128):
            for r in range(rows // 128):
                block = pl.program_id(0) * (rows // 128) + r
                out_ref[r * 128 : (r + 1) * 128, at : at + 128] = (
                    q_ref[r * 128 : (r + 1) * 128, c * 128 : (c + 1) * 128].astype(F32)
                    * scale_ref[block, c]
                ).astype(BF)
            at += 128


def scaled(pairs):
    rows, cols = pairs[0][0].shape
    tile = 256
    return pl.pallas_call(
        scale_kernel,
        grid=(rows // tile,),
        in_specs=[pl.BlockSpec(memory_space=pltpu.SMEM)] * len(pairs)
        + [pl.BlockSpec((tile, cols), lambda i: (i, 0))] * len(pairs),
        out_specs=pl.BlockSpec((tile, cols * len(pairs)), lambda i: (i, 0)),
        out_shape=jax.ShapeDtypeStruct((rows, cols * len(pairs)), BF),
        compiler_params=params(),
        name="scaled",
    )(*[s.astype(F32) for _, s in pairs], *[q for q, _ in pairs])


def slots_of(info, low, stride, at, k):
    local = info[:, k : k + 1] - low
    here = (local >= 0.0) & (local < float(NY * NC))
    return jnp.where(here, local * float(stride) + info[:, TOP + k : TOP + k + 1] + at, -1.0)


def dispatch_kernel(places, rows, based, z_at, *refs):
    count = len(places)
    chunks, routes = refs[:count], refs[count : 2 * count]
    out_ref, pick_ref, chunk_ref = refs[-3:]
    half = chunks[0].shape[0]

    @pl.when(pl.program_id(0) == 0)
    def _():
        low = (z_at[0] * (NY * NC)).astype(F32)
        for n, at in enumerate(places):
            info = routes[n][...].astype(F32)
            slots = lax.broadcasted_iota(jnp.int32, (half, pick_ref.shape[1]), 1).astype(F32)
            pick = jnp.zeros(slots.shape, F32)
            for k in range(TOP):
                pick = jnp.where(slots_of(info, low, rows, at, k) == slots, 1.0, pick)
            pick_ref[n * half : (n + 1) * half, :] = pick.astype(BF)

    for n, ref in enumerate(chunks):
        chunk_ref[n * half : (n + 1) * half, :] = ref[...]
    total = lax.dot_general(
        pick_ref[...], chunk_ref[...], (((0,), (0,)), ((), ())), preferred_element_type=F32
    )
    if based:
        total = total + refs[2 * count][...].astype(F32)
    out_ref[...] = total.astype(BF)


def dispatch(z_at, chunks, places, rows, base):
    plane = NY * NC
    half = chunks[0].shape[0]
    width = chunks[0].shape[1] - LANES
    tile = min(1024, width)
    bases = [] if base is None else [base]
    out_spec = pl.BlockSpec((plane * rows, tile), lambda i, z: (0, i))
    return pl.pallas_call(
        functools.partial(dispatch_kernel, places, rows, bool(bases)),
        grid_spec=pltpu.PrefetchScalarGridSpec(
            num_scalar_prefetch=1,
            grid=(width // tile,),
            in_specs=[pl.BlockSpec((half, tile), lambda i, z: (0, i))] * len(chunks)
            + [pl.BlockSpec((half, LANES), lambda i, z: (0, width // LANES))] * len(chunks)
            + [out_spec] * len(bases),
            out_specs=out_spec,
            scratch_shapes=[
                pltpu.VMEM((len(chunks) * half, plane * rows), BF),
                pltpu.VMEM((len(chunks) * half, tile), BF),
            ],
        ),
        out_shape=jax.ShapeDtypeStruct((plane * rows, width), BF),
        compiler_params=params(),
        name="dispatch",
    )(z_at, *chunks, *chunks, *bases)


def mixing_kernel(places, stride, z_at, *refs):
    routes, out_ref = refs[:-1], refs[-1]
    half = routes[0].shape[0]
    low = (z_at[0] * (NY * NC)).astype(F32)
    for n, at in enumerate(places):
        info = routes[n][...].astype(F32)
        slots = lax.broadcasted_iota(jnp.int32, (half, out_ref.shape[1]), 1).astype(F32)
        mix = jnp.zeros(slots.shape, F32)
        for k in range(TOP):
            weight = info[:, 2 * TOP + k : 2 * TOP + k + 1]
            mix = jnp.where(slots_of(info, low, stride, at, k) == slots, weight, mix)
        out_ref[n * half : (n + 1) * half, :] = mix.astype(BF)


def mixing(z_at, chunks, places, stride):
    half, width = chunks[0].shape
    return pl.pallas_call(
        functools.partial(mixing_kernel, places, stride),
        grid_spec=pltpu.PrefetchScalarGridSpec(
            num_scalar_prefetch=1,
            grid=(1,),
            in_specs=[pl.BlockSpec((half, LANES), lambda i, z: (0, width // LANES - 1))]
            * len(chunks),
            out_specs=pl.BlockSpec((len(chunks) * half, NY * NC * stride), lambda i, z: (0, 0)),
        ),
        out_shape=jax.ShapeDtypeStruct((len(chunks) * half, NY * NC * stride), BF),
        compiler_params=params(),
        name="mixing",
    )(z_at, *chunks)


def hidden_kernel(rows_ref, gate_ref, up_ref, out_ref):
    gate = jnp.dot(rows_ref[...], gate_ref[...], preferred_element_type=F32)
    up = jnp.dot(rows_ref[...], up_ref[...], preferred_element_type=F32)
    out_ref[...] = (gate / (1.0 + jnp.exp(-gate)) * up).astype(BF)


def hidden_units(rows, both):
    count, width = rows.shape
    units = both.shape[1] // 2
    tile = 256
    steps = units // tile
    return pl.pallas_call(
        hidden_kernel,
        grid=(steps,),
        in_specs=[
            pl.BlockSpec((count, width), lambda i: (0, 0)),
            pl.BlockSpec((width, tile), lambda i: (0, i)),
            pl.BlockSpec((width, tile), lambda i: (0, i + steps)),
        ],
        out_specs=pl.BlockSpec((count, tile), lambda i: (0, i)),
        out_shape=jax.ShapeDtypeStruct((count, units), BF),
        compiler_params=params(),
        name="hidden_units",
    )(rows, both, both)


def down_kernel(counts, hidden_ref, *refs):
    weights, out_ref = list(refs[:-1]), refs[-1]
    left = 0
    for count in counts:
        pieces, weights = weights[:count], weights[count:]
        width = pieces[0].shape[1]
        tile = min(512, width)
        for t in range(width // tile):
            at, total = 0, None
            for ref in pieces:
                part = jnp.dot(
                    hidden_ref[:, at : at + ref.shape[0]],
                    ref[:, t * tile : (t + 1) * tile],
                    preferred_element_type=F32,
                )
                total = part if total is None else total + part
                at += ref.shape[0]
            out_ref[:, left : left + tile] = total.astype(BF)
            left += tile


def project_down(hidden, slices):
    width = sum(s[0].shape[1] for s in slices)
    return pl.pallas_call(
        functools.partial(down_kernel, [len(s) for s in slices]),
        out_shape=jax.ShapeDtypeStruct((hidden.shape[0], width), BF),
        compiler_params=params(),
        name="project_down",
    )(hidden, *[w for s in slices for w in s])


def combine_kernel(rows_ref, mix_ref, *outs):
    at = 0
    for out_ref in outs:
        out_ref[...] = jnp.dot(
            mix_ref[at : at + out_ref.shape[0], :], rows_ref[...], preferred_element_type=F32
        ).astype(BF)
        at += out_ref.shape[0]


def combine(rows, mix, sizes):
    count, width = rows.shape
    tile = min(512, width)
    return pl.pallas_call(
        combine_kernel,
        grid=(width // tile,),
        in_specs=[
            pl.BlockSpec((count, tile), lambda i: (0, i)),
            pl.BlockSpec(mix.shape, lambda i: (0, 0)),
        ],
        out_specs=[pl.BlockSpec((m, tile), lambda i: (0, i)) for m in sizes],
        out_shape=[jax.ShapeDtypeStruct((m, width), BF) for m in sizes],
        compiler_params=params(),
        name="combine",
    )(rows, mix)


def join_kernel(ahead_ref, behind_ref, up_ref, down_ref, ahead_out, behind_out):
    size, half = ahead_ref.shape[0], up_ref.shape[0]
    for here, came, at, out in (
        (ahead_ref, up_ref, 0, ahead_out),
        (behind_ref, down_ref, size - half, behind_out),
    ):
        if half < size:
            out[...] = here[...]
        out[at : at + half, :] = (
            here[at : at + half, :].astype(F32) + came[...].astype(F32)
        ).astype(BF)


def join(ahead, behind, up, down):
    return pl.pallas_call(
        join_kernel,
        out_shape=[jax.ShapeDtypeStruct(ahead.shape, BF)] * 2,
        compiler_params=params(),
        name="join",
    )(ahead, behind, up, down)


def finish_kernel(offsets, x_at, *refs):
    parts, out_ref = refs[:-1], refs[-1]
    width = out_ref.shape[1] // NX
    own = x_at[0]
    for n, slices in enumerate(offsets):
        kept, ahead, behind = parts[3 * n : 3 * n + 3]
        for i, offset in enumerate(slices):
            cols = slice(i * width, (i + 1) * width)
            total = (
                kept[:, cols].astype(F32) + ahead[:, cols].astype(F32) + behind[:, cols].astype(F32)
            )
            place = pl.multiple_of(lax.rem(own + offset, NX) * width, 128)
            out_ref[:, pl.ds(place, width)] = total.astype(BF)


def finish(x_at, parts, offsets):
    rows = parts[0].shape[0]
    width = sum(p.shape[1] for p in parts[::3])
    return pl.pallas_call(
        functools.partial(finish_kernel, offsets),
        grid_spec=pltpu.PrefetchScalarGridSpec(
            num_scalar_prefetch=1,
            grid=(1,),
            in_specs=[pl.BlockSpec(p.shape, lambda i, s: (0, 0)) for p in parts],
            out_specs=pl.BlockSpec((rows, width), lambda i, s: (0, 0)),
        ),
        out_shape=jax.ShapeDtypeStruct((rows, width), BF),
        compiler_params=params(),
        name="finish",
    )(x_at, *parts)


def body(
    tokens,
    norm_gain,
    route_ids,
    route_weights,
    gate_q,
    gate_scale,
    up_q,
    up_scale,
    down_q,
    down_scale,
):
    tok_rows, width = tokens.shape
    units = down_q.shape[1]
    assert tok_rows == TOK and route_ids.shape[1] == TOP
    half = tok_rows // 2
    plane = NY * NC
    z_at = jnp.reshape(lax.axis_index("z"), (1,)).astype(jnp.int32)
    x_at = jnp.reshape(lax.axis_index("x"), (1,)).astype(jnp.int32)

    both = scaled([(gate_q[0], gate_scale[0]), (up_q[0], up_scale[0])])
    (tokens,) = after((tokens,), (both,))
    both = lax.all_gather(both, "x", axis=0, tiled=True)

    chunks = {0: prepare(tokens, norm_gain, route_ids, route_weights)}
    for step in (1, 2, 3):
        chunks[-step] = [shift(a, "z", NZ, 1) for a in chunks[1 - step]]
        chunks[step] = [shift(a, "z", NZ, -1) for a in chunks[step - 1]]
    chunks[4] = [shift(chunks[-3][0], "z", NZ, 1), shift(chunks[3][1], "z", NZ, -1)]

    down_own = scaled([(down_q[0], down_scale[0])])
    (down_own,) = after((down_own,), chunks[DOWN_AFTER])
    low, high = shift(down_own, "x", NX, 1), shift(down_own, "x", NX, -1)
    far = [
        shift(low[: units // 2], "x", NX, 1),
        shift(high[units // 2 :], "x", NX, -1),
    ]

    stride = CAP * NZ
    hidden, start, at_mix = [], 0, {}
    for group in GROUPS:
        rows = -(-CAP * sum(len(stage) for stage in group) // 8) * 8
        blocks, used = None, 0
        for stage in group:
            arrays, places = [], []
            for j in stage:
                arrays += chunks[j]
                places += [float(used)] * 2
                at_mix[j] = float(start + used)
                used += CAP
            blocks = dispatch(z_at, arrays, places, rows, blocks)
        rows_in = exchange(blocks.reshape(plane, rows, width)).reshape(plane * rows, width)
        units_out = hidden_units(rows_in, both)
        hidden.append(units_out.reshape(plane, rows, units)[:, :used])
        start += used
    hidden = jnp.concatenate(hidden, axis=1).reshape(plane * stride, units)

    order = (4, 3, -3, 2, -2, 1, -1, 0)
    mix = mixing(
        z_at, [a for j in order for a in chunks[j]], [at_mix[j] for j in order for _ in (0, 1)], stride
    )
    sizes = [half, half] + [tok_rows] * (NZ - 1)

    finals, sums, held = [], (), ()
    for weights in SLICES:
        weights = [{"own": [down_own], "low": [low], "high": [high], "far": far}[w] for w in weights]
        (out,) = after((project_down(hidden, weights),), sums)
        cols = out.shape[1]
        back = exchange(out.reshape(plane, stride, cols)).reshape(plane * stride, cols)
        (back,) = after((back,), held)
        sums = combine(back, mix, sizes)
        ahead, behind = shift(sums[0], "z", NZ, 1), shift(sums[1], "z", NZ, -1)
        for step in (2, 4, 6):
            ahead, behind = join(sums[step], sums[step + 1], ahead, behind)
            ahead, behind = shift(ahead, "z", NZ, 1), shift(behind, "z", NZ, -1)
            if step == HOLD:
                held = (ahead, behind)
        finals += [sums[8], ahead, behind]
    offsets = [[{"own": 0, "low": NX - 1, "high": 1, "far": 2}[w] for w in s] for s in SLICES]
    return finish(x_at, finals, offsets)


def solution(mesh):
    assert mesh.devices.shape == (NZ * NY * NC, NX)
    fine = Mesh(mesh.devices.reshape(NZ, NY, NC, NX), ("z", "y", "core", "x"))
    expert = ("z", "y", "core")
    every = ("z", "y", "core", "x")
    in_specs = (
        P(every, None),
        P(),
        P(every, None),
        P(every, None),
        P(expert, "x", None),
        P(expert, "x", None),
        P(expert, "x", None),
        P(expert, "x", None),
        P(expert, None, "x"),
        P(expert, None, "x"),
    )
    return jax.shard_map(
        body, mesh=fine, in_specs=in_specs, out_specs=P(every, None), check_vma=False
    )
```

```python
import functools

import jax
import jax.numpy as jnp
from jax import lax
from jax.experimental import pallas as pl
from jax.experimental.pallas import tpu as pltpu
from jax.sharding import Mesh
from jax.sharding import PartitionSpec as P

BF = jnp.bfloat16
F32 = jnp.float32
VMEM_LIMIT = 52 * 1024 * 1024
CAP = 10
TOK, TOP = 128, 4
LANES = 128
NZ, NY, NC, NX = 8, 4, 2, 4
PLANE = NY * NC
STRIDE = CAP * NZ
PARTS = {"own": 0, "low": NX - 1, "high": 1, "far": 2}
SLICES = (("own",), ("low", "high"), ("far",))
HOLDS = (4, 2, None)


def params(**kw):
    return pltpu.CompilerParams(vmem_limit_bytes=VMEM_LIMIT, **kw)


def shift(array, axis, size, by):
    return lax.ppermute(array, axis, [(i, (i + by) % size) for i in range(size)])


def exchange(blocks):
    return lax.all_to_all(blocks, ("y", "core"), split_axis=0, concat_axis=0, tiled=True)


def after(arrays, earlier):
    return lax.optimization_barrier((tuple(arrays), tuple(earlier)))[0]


def prepare_kernel(x_at, tok_ref, gain_ref, ids_ref, weights_ref, *outs):
    rows = tok_ref.shape[0]
    width = outs[-1].shape[1]
    values = tok_ref[...].astype(F32)
    mean_square = jnp.mean(values * values, axis=-1, keepdims=True)
    scale = lax.rsqrt(mean_square + 1e-06)
    for offset, out_ref in zip(PARTS.values(), outs):
        cols = pl.ds(pl.multiple_of(lax.rem(x_at[0] + offset, NX) * width, 128), width)
        out_ref[:, :width] = (
            tok_ref[:, cols].astype(F32) * scale * gain_ref[:, cols].astype(F32)
        ).astype(BF)
    experts = lax.broadcasted_iota(jnp.int32, (rows, LANES), 1)
    chosen = [(ids_ref[:, k : k + 1] == experts).astype(F32) for k in range(TOP)]
    counts = sum(chosen).astype(BF)
    earlier = (
        lax.broadcasted_iota(jnp.int32, (rows, rows), 0)
        > lax.broadcasted_iota(jnp.int32, (rows, rows), 1)
    )
    before = jnp.dot(earlier.astype(F32).astype(BF), counts, preferred_element_type=F32)
    lane = lax.broadcasted_iota(jnp.int32, (rows, LANES), 1)
    routes = jnp.zeros((rows, LANES), F32)
    for k in range(TOP):
        rank = jnp.sum(chosen[k] * before, axis=1, keepdims=True)
        routes = jnp.where(lane == k, ids_ref[:, k : k + 1].astype(F32), routes)
        routes = jnp.where(lane == TOP + k, rank, routes)
        routes = jnp.where(lane == 2 * TOP + k, weights_ref[:, k : k + 1].astype(F32), routes)
    outs[0][:, width:] = routes.astype(BF)


def prepare(x_at, tokens, gain, ids, weights):
    rows, width = tokens.shape
    quarter = width // NX
    widths = [quarter + LANES] + [quarter] * (NX - 1)

    def whole(shape):
        return pl.BlockSpec(shape, lambda i, s: (0, 0))

    return pl.pallas_call(
        prepare_kernel,
        grid_spec=pltpu.PrefetchScalarGridSpec(
            num_scalar_prefetch=1,
            grid=(1,),
            in_specs=[whole((rows, width)), whole((1, width)), whole(ids.shape), whole(ids.shape)],
            out_specs=[whole((rows, w)) for w in widths],
        ),
        out_shape=[jax.ShapeDtypeStruct((rows, w), BF) for w in widths],
        compiler_params=params(),
        name="prepare",
    )(x_at, tokens, gain.reshape(1, width), ids, weights)


def scale_kernel(first, *refs):
    count = (len(refs) - 1) // 2
    scales, values, out_ref = refs[:count], refs[count : 2 * count], refs[-1]
    rows = values[0].shape[0]
    at = 0
    for scale_ref, q_ref in zip(scales, values):
        for c in range(q_ref.shape[1] // 128):
            for r in range(rows // 128):
                block = pl.program_id(0) * (rows // 128) + r + first
                out_ref[r * 128 : (r + 1) * 128, at : at + 128] = (
                    q_ref[r * 128 : (r + 1) * 128, c * 128 : (c + 1) * 128].astype(F32)
                    * scale_ref[block, c]
                ).astype(BF)
            at += 128


def scaled(pairs, part, parts):
    rows, cols = pairs[0][0].shape
    tile = 128
    steps = rows // parts // tile
    first = part * steps
    return pl.pallas_call(
        functools.partial(scale_kernel, first * (tile // 128)),
        grid=(steps,),
        in_specs=[pl.BlockSpec(memory_space=pltpu.SMEM)] * len(pairs)
        + [pl.BlockSpec((tile, cols), lambda i: (i + first, 0))] * len(pairs),
        out_specs=pl.BlockSpec((tile, cols * len(pairs)), lambda i: (i, 0)),
        out_shape=jax.ShapeDtypeStruct((rows // parts, cols * len(pairs)), BF),
        compiler_params=params(),
        name="scaled",
    )(*[s.astype(F32) for _, s in pairs], *[q for q, _ in pairs])


def select_kernel(z_at, routes_ref, pick_ref, mix_ref):
    low = (z_at[0] * PLANE).astype(F32)
    base = (pl.program_id(0) * CAP).astype(F32)
    info = routes_ref[...].astype(F32)
    slots = lax.broadcasted_iota(jnp.int32, mix_ref.shape, 1).astype(F32)
    pick = jnp.zeros(slots.shape, F32)
    mix = jnp.zeros(slots.shape, F32)
    for k in range(TOP):
        local = info[:, k : k + 1] - low
        here = (local >= 0.0) & (local < float(PLANE))
        slot = local * float(STRIDE) + info[:, TOP + k : TOP + k + 1] + base
        same = jnp.where(here, slot, -1.0) == slots
        pick = jnp.where(same, 1.0, pick)
        mix = jnp.where(same, info[:, 2 * TOP + k : 2 * TOP + k + 1], mix)
    pick_ref[...] = pick.T.astype(BF)
    mix_ref[...] = mix.astype(BF)


def select(z_at, first):
    rows, width = first.shape
    slots = PLANE * STRIDE
    return pl.pallas_call(
        select_kernel,
        grid_spec=pltpu.PrefetchScalarGridSpec(
            num_scalar_prefetch=1,
            grid=(NZ,),
            in_specs=[pl.BlockSpec((TOK, LANES), lambda i, z: (i, width // LANES - 1))],
            out_specs=[
                pl.BlockSpec((slots, TOK), lambda i, z: (0, i)),
                pl.BlockSpec((TOK, slots), lambda i, z: (i, 0)),
            ],
        ),
        out_shape=[
            jax.ShapeDtypeStruct((slots, rows), BF),
            jax.ShapeDtypeStruct((rows, slots), BF),
        ],
        compiler_params=params(),
        name="select",
    )(z_at, first)


def dispatch_kernel(pick_ref, rows_ref, out_ref):
    out_ref[...] = jnp.dot(pick_ref[...], rows_ref[...], preferred_element_type=F32).astype(BF)


def dispatch(pick, rows, width):
    tile = min(512, width)
    return pl.pallas_call(
        dispatch_kernel,
        grid=(width // tile,),
        in_specs=[
            pl.BlockSpec(pick.shape, lambda i: (0, 0)),
            pl.BlockSpec((rows.shape[0], tile), lambda i: (0, i)),
        ],
        out_specs=pl.BlockSpec((pick.shape[0], tile), lambda i: (0, i)),
        out_shape=jax.ShapeDtypeStruct((pick.shape[0], width), BF),
        compiler_params=params(),
        name="dispatch",
    )(pick, rows)


def gather_sum(rows, pieces, total):
    pieces = list(pieces)
    for ref in rows:
        at = 0
        while at < ref.shape[1]:
            piece = pieces.pop(0)
            depth = piece.shape[0]
            part = jnp.dot(ref[:, at : at + depth], piece[...], preferred_element_type=F32)
            total = part if total is None else total + part
            at += depth
    return total


def early_kernel(blocks, count, *refs):
    rows, gates, ups = refs[:blocks], refs[blocks : blocks + count], refs[blocks + count : -2]
    refs[-2][...] = gather_sum(rows, gates, None)
    refs[-1][...] = gather_sum(rows, ups, None)


def late_kernel(blocks, count, *refs):
    rows, gates = refs[:blocks], refs[blocks : blocks + count]
    ups = refs[blocks + count : blocks + 2 * count]
    gate = gather_sum(rows, gates, refs[-3][...])
    up = gather_sum(rows, ups, refs[-2][...])
    refs[-1][...] = (gate / (1.0 + jnp.exp(-gate)) * up).astype(BF)


def hidden_units(rows, pieces, sums):
    count = rows[0].shape[0]
    units = pieces[0].shape[1] // 2
    tile = 256
    steps = units // tile
    out_spec = pl.BlockSpec((count, tile), lambda i: (0, i))
    kernel = late_kernel if sums else early_kernel
    return pl.pallas_call(
        functools.partial(kernel, len(rows), len(pieces)),
        grid=(steps,),
        in_specs=[pl.BlockSpec(r.shape, lambda i: (0, 0)) for r in rows]
        + [pl.BlockSpec((w.shape[0], tile), lambda i: (0, i)) for w in pieces]
        + [pl.BlockSpec((w.shape[0], tile), lambda i: (0, i + steps)) for w in pieces]
        + [out_spec] * len(sums),
        out_specs=out_spec if sums else [out_spec] * 2,
        out_shape=jax.ShapeDtypeStruct((count, units), BF)
        if sums
        else [jax.ShapeDtypeStruct((count, units), F32)] * 2,
        compiler_params=params(),
        name="hidden_units" if sums else "early_sums",
    )(*rows, *pieces, *pieces, *sums)


def down_kernel(counts, hidden_ref, *refs):
    weights, out_ref = list(refs[:-1]), refs[-1]
    left = 0
    for count in counts:
        pieces, weights = weights[:count], weights[count:]
        width = pieces[0].shape[1]
        tile = min(512, width)
        for t in range(width // tile):
            at, total = 0, None
            for ref in pieces:
                part = jnp.dot(
                    hidden_ref[:, at : at + ref.shape[0]],
                    ref[:, t * tile : (t + 1) * tile],
                    preferred_element_type=F32,
                )
                total = part if total is None else total + part
                at += ref.shape[0]
            out_ref[:, left : left + tile] = total.astype(BF)
            left += tile


def project_down(hidden, slices):
    width = sum(s[0].shape[1] for s in slices)
    return pl.pallas_call(
        functools.partial(down_kernel, [len(s) for s in slices]),
        out_shape=jax.ShapeDtypeStruct((hidden.shape[0], width), BF),
        compiler_params=params(),
        name="project_down",
    )(hidden, *[w for s in slices for w in s])


def combine_kernel(order, z_at, rows_ref, mix_ref, *outs):
    half = TOK // 2
    for (offset, at), out_ref in zip(order, outs):
        place = lax.rem(z_at[0] + offset, NZ) * TOK + at
        mix = mix_ref[pl.ds(pl.multiple_of(place, half), out_ref.shape[0]), :]
        out_ref[...] = jnp.dot(mix, rows_ref[...], preferred_element_type=F32).astype(BF)


def combine(z_at, rows, mix):
    count, width = rows.shape
    tile = min(512, width)
    order = [(4, 0), (4, TOK // 2)] + [(j, 0) for j in (3, NZ - 3, 2, NZ - 2, 1, NZ - 1, 0)]
    sizes = [TOK // 2] * 2 + [TOK] * (NZ - 1)
    return pl.pallas_call(
        functools.partial(combine_kernel, order),
        grid_spec=pltpu.PrefetchScalarGridSpec(
            num_scalar_prefetch=1,
            grid=(width // tile,),
            in_specs=[
                pl.BlockSpec((count, tile), lambda i, z: (0, i)),
                pl.BlockSpec(mix.shape, lambda i, z: (0, 0)),
            ],
            out_specs=[pl.BlockSpec((m, tile), lambda i, z: (0, i)) for m in sizes],
        ),
        out_shape=[jax.ShapeDtypeStruct((m, width), BF) for m in sizes],
        compiler_params=params(),
        name="combine",
    )(z_at, rows, mix)


def join_kernel(ahead_ref, behind_ref, up_ref, down_ref, ahead_out, behind_out):
    size, half = ahead_ref.shape[0], up_ref.shape[0]
    for here, came, at, out in (
        (ahead_ref, up_ref, 0, ahead_out),
        (behind_ref, down_ref, size - half, behind_out),
    ):
        if half < size:
            out[...] = here[...]
        out[at : at + half, :] = (
            here[at : at + half, :].astype(F32) + came[...].astype(F32)
        ).astype(BF)


def join(ahead, behind, up, down):
    return pl.pallas_call(
        join_kernel,
        out_shape=[jax.ShapeDtypeStruct(ahead.shape, BF)] * 2,
        compiler_params=params(),
        name="join",
    )(ahead, behind, up, down)


def finish_kernel(offsets, x_at, *refs):
    parts, out_ref = refs[:-1], refs[-1]
    width = out_ref.shape[1] // NX
    own = x_at[0]
    for n, slices in enumerate(offsets):
        kept, ahead, behind = parts[3 * n : 3 * n + 3]
        for i, offset in enumerate(slices):
            cols = slice(i * width, (i + 1) * width)
            total = (
                kept[:, cols].astype(F32) + ahead[:, cols].astype(F32) + behind[:, cols].astype(F32)
            )
            place = pl.multiple_of(lax.rem(own + offset, NX) * width, 128)
            out_ref[:, pl.ds(place, width)] = total.astype(BF)


def finish(x_at, parts, offsets):
    rows = parts[0].shape[0]
    width = sum(p.shape[1] for p in parts[::3])
    return pl.pallas_call(
        functools.partial(finish_kernel, offsets),
        grid_spec=pltpu.PrefetchScalarGridSpec(
            num_scalar_prefetch=1,
            grid=(1,),
            in_specs=[pl.BlockSpec(p.shape, lambda i, s: (0, 0)) for p in parts],
            out_specs=pl.BlockSpec((rows, width), lambda i, s: (0, 0)),
        ),
        out_shape=jax.ShapeDtypeStruct((rows, width), BF),
        compiler_params=params(),
        name="finish",
    )(x_at, *parts)


def body(
    tokens,
    norm_gain,
    route_ids,
    route_weights,
    gate_q,
    gate_scale,
    up_q,
    up_scale,
    down_q,
    down_scale,
):
    tok_rows, width = tokens.shape
    units = down_q.shape[1]
    quarter = width // NX
    assert tok_rows == TOK and route_ids.shape[1] == TOP
    z_at = jnp.reshape(lax.axis_index("z"), (1,)).astype(jnp.int32)
    x_at = jnp.reshape(lax.axis_index("x"), (1,)).astype(jnp.int32)

    own = list(prepare(x_at, tokens, norm_gain, route_ids, route_weights))
    gate_q, up_q = after((gate_q, up_q), own)
    pairs = [(gate_q[0], gate_scale[0]), (up_q[0], up_scale[0])]
    top, bottom = scaled(pairs, 0, 2), scaled(pairs, 1, 2)
    low_top, high_bottom = shift(top, "x", NX, 1), shift(bottom, "x", NX, -1)
    up, down = after((bottom, top), (low_top, high_bottom))
    low_bottom, high_top = shift(up, "x", NX, 1), shift(down, "x", NX, -1)
    up, down = after((low_top, high_bottom), (low_bottom, high_top))
    far = [shift(up, "x", NX, 1), shift(down, "x", NX, -1)]
    early = [top, bottom, low_top, low_bottom, high_top, high_bottom]

    down_own = scaled([(down_q[0], down_scale[0])], 0, 1)
    (down_own,) = after((down_own,), far)
    down_low, down_high = shift(down_own, "x", NX, 1), shift(down_own, "x", NX, -1)
    downs = {
        "own": [down_own],
        "low": [down_low],
        "high": [down_high],
        "far": [
            shift(down_low[: units // 2], "x", NX, 1),
            shift(down_high[units // 2 :], "x", NX, -1),
        ],
    }

    (own[2],) = after((own[2],), (low_top, high_bottom))
    (own[3],) = after((own[3],), (low_bottom, high_top))
    gathered = [lax.all_gather(a, "z", axis=0, tiled=True) for a in own]
    pick, mix = select(z_at, gathered[0])
    rows_in = []
    for a in gathered:
        blocks = dispatch(pick, a, quarter).reshape(PLANE, STRIDE, quarter)
        rows_in.append(exchange(blocks).reshape(PLANE * STRIDE, quarter))

    sums = hidden_units(rows_in[:3], early, ())
    hidden = hidden_units(rows_in[3:], far, sums)

    finals, sums, held = [], (), ()
    for names, hold in zip(SLICES, HOLDS):
        (out,) = after((project_down(hidden, [downs[n] for n in names]),), sums)
        cols = out.shape[1]
        back = exchange(out.reshape(PLANE, STRIDE, cols)).reshape(PLANE * STRIDE, cols)
        (back,) = after((back,), held)
        sums = combine(z_at, back, mix)
        ahead, behind = shift(sums[0], "z", NZ, 1), shift(sums[1], "z", NZ, -1)
        for step in (2, 4, 6):
            ahead, behind = join(sums[step], sums[step + 1], ahead, behind)
            ahead, behind = shift(ahead, "z", NZ, 1), shift(behind, "z", NZ, -1)
            if step == hold:
                held = (ahead, behind)
        finals += [sums[8], ahead, behind]
    return finish(x_at, finals, [[PARTS[n] for n in names] for names in SLICES])


def solution(mesh):
    assert mesh.devices.shape == (NZ * NY * NC, NX)
    fine = Mesh(mesh.devices.reshape(NZ, NY, NC, NX), ("z", "y", "core", "x"))
    expert = ("z", "y", "core")
    every = ("z", "y", "core", "x")
    in_specs = (
        P(every, None),
        P(),
        P(every, None),
        P(every, None),
        P(expert, "x", None),
        P(expert, "x", None),
        P(expert, "x", None),
        P(expert, "x", None),
        P(expert, None, "x"),
        P(expert, None, "x"),
    )
    return jax.shard_map(
        body, mesh=fine, in_specs=in_specs, out_specs=P(every, None), check_vma=False
    )
```

```python
import functools

import jax
import jax.numpy as jnp
from jax import lax
from jax.experimental import pallas as pl
from jax.experimental.pallas import tpu as pltpu
from jax.sharding import Mesh
from jax.sharding import PartitionSpec as P

BF = jnp.bfloat16
F32 = jnp.float32
VMEM_LIMIT = 52 * 1024 * 1024
CAP = 10
TOK, TOP = 128, 4
LANES = 128
SLICES = (("own", "low"), ("high", "far"))
SPLIT = 2
FORCE = True
HOLD = 2
DOWN_AFTER = 2
NZ, NY, NC, NX = 8, 4, 2, 4
GROUPS = (((0, -1, 1), (-2, 2)), ((-3, 3), (4,)))


def params(**kw):
    return pltpu.CompilerParams(vmem_limit_bytes=VMEM_LIMIT, **kw)


def shift(array, axis, size, by):
    return lax.ppermute(array, axis, [(i, (i + by) % size) for i in range(size)])


def exchange(blocks):
    return lax.all_to_all(blocks, ("y", "core"), split_axis=0, concat_axis=0, tiled=True)


def after(arrays, earlier):
    return lax.optimization_barrier((tuple(arrays), tuple(earlier)))[0]


def prepare_kernel(tok_ref, gain_ref, ids_ref, weights_ref, *outs):
    rows, width = tok_ref.shape
    half = rows // 2
    top = ids_ref.shape[1]
    experts = lax.broadcasted_iota(jnp.int32, (rows, LANES), 1)
    chosen = [(ids_ref[:, k : k + 1] == experts).astype(F32) for k in range(top)]
    counts = sum(chosen).astype(BF)
    earlier = (
        lax.broadcasted_iota(jnp.int32, (rows, rows), 0)
        > lax.broadcasted_iota(jnp.int32, (rows, rows), 1)
    )
    before = jnp.dot(earlier.astype(F32).astype(BF), counts, preferred_element_type=F32)
    lane = lax.broadcasted_iota(jnp.int32, (rows, LANES), 1)
    routes = jnp.zeros((rows, LANES), F32)
    for k in range(top):
        rank = jnp.sum(chosen[k] * before, axis=1, keepdims=True)
        routes = jnp.where(lane == k, ids_ref[:, k : k + 1].astype(F32), routes)
        routes = jnp.where(lane == top + k, rank, routes)
        routes = jnp.where(lane == 2 * top + k, weights_ref[:, k : k + 1].astype(F32), routes)
    routes = routes.astype(BF)
    for n, out_ref in enumerate(outs):
        values = tok_ref[n * half : (n + 1) * half, :].astype(F32)
        mean_square = jnp.mean(values * values, axis=-1, keepdims=True)
        out_ref[:, :width] = (
            values * lax.rsqrt(mean_square + 1e-06) * gain_ref[...].astype(F32)
        ).astype(BF)
        out_ref[:, width:] = routes[n * half : (n + 1) * half]


def prepare(tokens, gain, ids, weights):
    rows, width = tokens.shape
    half = jax.ShapeDtypeStruct((rows // 2, width + LANES), BF)
    return pl.pallas_call(
        prepare_kernel,
        out_shape=[half, half],
        compiler_params=params(),
        name="prepare",
    )(tokens, gain.reshape(1, width), ids, weights)


def scale_kernel(*refs):
    count = (len(refs) - 1) // 2
    scales, values, out_ref = refs[:count], refs[count : 2 * count], refs[-1]
    rows = values[0].shape[0]
    at = 0
    for scale_ref, q_ref in zip(scales, values):
        for c in range(q_ref.shape[1] // 128):
            for r in range(rows // 128):
                block = pl.program_id(0) * (rows // 128) + r
                out_ref[r * 128 : (r + 1) * 128, at : at + 128] = (
                    q_ref[r * 128 : (r + 1) * 128, c * 128 : (c + 1) * 128].astype(F32)
                    * scale_ref[block, c]
                ).astype(BF)
            at += 128


def scaled(pairs):
    rows, cols = pairs[0][0].shape
    tile = 256
    return pl.pallas_call(
        scale_kernel,
        grid=(rows // tile,),
        in_specs=[pl.BlockSpec(memory_space=pltpu.SMEM)] * len(pairs)
        + [pl.BlockSpec((tile, cols), lambda i: (i, 0))] * len(pairs),
        out_specs=pl.BlockSpec((tile, cols * len(pairs)), lambda i: (i, 0)),
        out_shape=jax.ShapeDtypeStruct((rows, cols * len(pairs)), BF),
        compiler_params=params(),
        name="scaled",
    )(*[s.astype(F32) for _, s in pairs], *[q for q, _ in pairs])


def slots_of(info, low, stride, at, k):
    local = info[:, k : k + 1] - low
    here = (local >= 0.0) & (local < float(NY * NC))
    return jnp.where(here, local * float(stride) + info[:, TOP + k : TOP + k + 1] + at, -1.0)


def dispatch_kernel(places, rows, based, z_at, *refs):
    count = len(places)
    chunks, routes = refs[:count], refs[count : 2 * count]
    out_ref, pick_ref, chunk_ref = refs[-3:]
    half = chunks[0].shape[0]

    @pl.when(pl.program_id(0) == 0)
    def _():
        low = (z_at[0] * (NY * NC)).astype(F32)
        for n, at in enumerate(places):
            info = routes[n][...].astype(F32)
            slots = lax.broadcasted_iota(jnp.int32, (half, pick_ref.shape[1]), 1).astype(F32)
            pick = jnp.zeros(slots.shape, F32)
            for k in range(TOP):
                pick = jnp.where(slots_of(info, low, rows, at, k) == slots, 1.0, pick)
            pick_ref[n * half : (n + 1) * half, :] = pick.astype(BF)

    for n, ref in enumerate(chunks):
        chunk_ref[n * half : (n + 1) * half, :] = ref[...]
    total = lax.dot_general(
        pick_ref[...], chunk_ref[...], (((0,), (0,)), ((), ())), preferred_element_type=F32
    )
    if based:
        total = total + refs[2 * count][...].astype(F32)
    out_ref[...] = total.astype(BF)


def dispatch(z_at, chunks, places, rows, base):
    plane = NY * NC
    half = chunks[0].shape[0]
    width = chunks[0].shape[1] - LANES
    tile = min(1024, width)
    bases = [] if base is None else [base]
    out_spec = pl.BlockSpec((plane * rows, tile), lambda i, z: (0, i))
    return pl.pallas_call(
        functools.partial(dispatch_kernel, places, rows, bool(bases)),
        grid_spec=pltpu.PrefetchScalarGridSpec(
            num_scalar_prefetch=1,
            grid=(width // tile,),
            in_specs=[pl.BlockSpec((half, tile), lambda i, z: (0, i))] * len(chunks)
            + [pl.BlockSpec((half, LANES), lambda i, z: (0, width // LANES))] * len(chunks)
            + [out_spec] * len(bases),
            out_specs=out_spec,
            scratch_shapes=[
                pltpu.VMEM((len(chunks) * half, plane * rows), BF),
                pltpu.VMEM((len(chunks) * half, tile), BF),
            ],
        ),
        out_shape=jax.ShapeDtypeStruct((plane * rows, width), BF),
        compiler_params=params(),
        name="dispatch",
    )(z_at, *chunks, *chunks, *bases)


def mixing_kernel(places, stride, z_at, *refs):
    routes, out_ref = refs[:-1], refs[-1]
    half = routes[0].shape[0]
    low = (z_at[0] * (NY * NC)).astype(F32)
    for n, at in enumerate(places):
        info = routes[n][...].astype(F32)
        slots = lax.broadcasted_iota(jnp.int32, (half, out_ref.shape[1]), 1).astype(F32)
        mix = jnp.zeros(slots.shape, F32)
        for k in range(TOP):
            weight = info[:, 2 * TOP + k : 2 * TOP + k + 1]
            mix = jnp.where(slots_of(info, low, stride, at, k) == slots, weight, mix)
        out_ref[n * half : (n + 1) * half, :] = mix.astype(BF)


def mixing(z_at, chunks, places, stride):
    half, width = chunks[0].shape
    return pl.pallas_call(
        functools.partial(mixing_kernel, places, stride),
        grid_spec=pltpu.PrefetchScalarGridSpec(
            num_scalar_prefetch=1,
            grid=(1,),
            in_specs=[pl.BlockSpec((half, LANES), lambda i, z: (0, width // LANES - 1))]
            * len(chunks),
            out_specs=pl.BlockSpec((len(chunks) * half, NY * NC * stride), lambda i, z: (0, 0)),
        ),
        out_shape=jax.ShapeDtypeStruct((len(chunks) * half, NY * NC * stride), BF),
        compiler_params=params(),
        name="mixing",
    )(z_at, *chunks)


def hidden_kernel(rows_ref, gate_ref, up_ref, out_ref):
    gate = jnp.dot(rows_ref[...], gate_ref[...], preferred_element_type=F32)
    up = jnp.dot(rows_ref[...], up_ref[...], preferred_element_type=F32)
    out_ref[...] = (gate / (1.0 + jnp.exp(-gate)) * up).astype(BF)


def hidden_units(rows, both):
    count, width = rows.shape
    units = both.shape[1] // 2
    tile = 256
    steps = units // tile
    return pl.pallas_call(
        hidden_kernel,
        grid=(steps,),
        in_specs=[
            pl.BlockSpec((count, width), lambda i: (0, 0)),
            pl.BlockSpec((width, tile), lambda i: (0, i)),
            pl.BlockSpec((width, tile), lambda i: (0, i + steps)),
        ],
        out_specs=pl.BlockSpec((count, tile), lambda i: (0, i)),
        out_shape=jax.ShapeDtypeStruct((count, units), BF),
        compiler_params=params(),
        name="hidden_units",
    )(rows, both, both)


def down_kernel(counts, hidden_ref, *refs):
    weights, out_ref = list(refs[:-1]), refs[-1]
    left = 0
    for count in counts:
        pieces, weights = weights[:count], weights[count:]
        width = pieces[0].shape[1]
        tile = min(512, width)
        for t in range(width // tile):
            at, total = 0, None
            for ref in pieces:
                part = jnp.dot(
                    hidden_ref[:, at : at + ref.shape[0]],
                    ref[:, t * tile : (t + 1) * tile],
                    preferred_element_type=F32,
                )
                total = part if total is None else total + part
                at += ref.shape[0]
            out_ref[:, left : left + tile] = total.astype(BF)
            left += tile


def project_down(hidden, slices):
    width = sum(s[0].shape[1] for s in slices)
    return pl.pallas_call(
        functools.partial(down_kernel, [len(s) for s in slices]),
        out_shape=jax.ShapeDtypeStruct((hidden.shape[0], width), BF),
        compiler_params=params(),
        name="project_down",
    )(hidden, *[w for s in slices for w in s])


def combine_kernel(rows_ref, mix_ref, *outs):
    at = 0
    for out_ref in outs:
        out_ref[...] = jnp.dot(
            mix_ref[at : at + out_ref.shape[0], :], rows_ref[...], preferred_element_type=F32
        ).astype(BF)
        at += out_ref.shape[0]


def combine(rows, mix, sizes, part, parts):
    count, width = rows.shape[0], rows.shape[1] // parts
    tile = min(512, width)
    first = part * (width // tile)
    return pl.pallas_call(
        combine_kernel,
        grid=(width // tile,),
        in_specs=[
            pl.BlockSpec((count, tile), lambda i: (0, i + first)),
            pl.BlockSpec(mix.shape, lambda i: (0, 0)),
        ],
        out_specs=[pl.BlockSpec((m, tile), lambda i: (0, i)) for m in sizes],
        out_shape=[jax.ShapeDtypeStruct((m, width), BF) for m in sizes],
        compiler_params=params(),
        name="combine",
    )(rows, mix)


def join_kernel(ahead_ref, behind_ref, up_ref, down_ref, ahead_out, behind_out):
    size, half = ahead_ref.shape[0], up_ref.shape[0]
    for here, came, at, out in (
        (ahead_ref, up_ref, 0, ahead_out),
        (behind_ref, down_ref, size - half, behind_out),
    ):
        if half < size:
            out[...] = here[...]
        out[at : at + half, :] = (
            here[at : at + half, :].astype(F32) + came[...].astype(F32)
        ).astype(BF)


def join(ahead, behind, up, down):
    return pl.pallas_call(
        join_kernel,
        out_shape=[jax.ShapeDtypeStruct(ahead.shape, BF)] * 2,
        compiler_params=params(),
        name="join",
    )(ahead, behind, up, down)


def finish_kernel(offsets, x_at, *refs):
    parts, out_ref = refs[:-1], refs[-1]
    width = out_ref.shape[1] // NX
    own = x_at[0]
    for n, slices in enumerate(offsets):
        kept, ahead, behind = parts[3 * n : 3 * n + 3]
        for i, offset in enumerate(slices):
            cols = slice(i * width, (i + 1) * width)
            total = (
                kept[:, cols].astype(F32) + ahead[:, cols].astype(F32) + behind[:, cols].astype(F32)
            )
            place = pl.multiple_of(lax.rem(own + offset, NX) * width, 128)
            out_ref[:, pl.ds(place, width)] = total.astype(BF)


def finish(x_at, parts, offsets):
    rows = parts[0].shape[0]
    width = sum(p.shape[1] for p in parts[::3])
    return pl.pallas_call(
        functools.partial(finish_kernel, offsets),
        grid_spec=pltpu.PrefetchScalarGridSpec(
            num_scalar_prefetch=1,
            grid=(1,),
            in_specs=[pl.BlockSpec(p.shape, lambda i, s: (0, 0)) for p in parts],
            out_specs=pl.BlockSpec((rows, width), lambda i, s: (0, 0)),
        ),
        out_shape=jax.ShapeDtypeStruct((rows, width), BF),
        compiler_params=params(),
        name="finish",
    )(x_at, *parts)


def body(
    tokens,
    norm_gain,
    route_ids,
    route_weights,
    gate_q,
    gate_scale,
    up_q,
    up_scale,
    down_q,
    down_scale,
):
    tok_rows, width = tokens.shape
    units = down_q.shape[1]
    assert tok_rows == TOK and route_ids.shape[1] == TOP
    half = tok_rows // 2
    plane = NY * NC
    z_at = jnp.reshape(lax.axis_index("z"), (1,)).astype(jnp.int32)
    x_at = jnp.reshape(lax.axis_index("x"), (1,)).astype(jnp.int32)

    both = scaled([(gate_q[0], gate_scale[0]), (up_q[0], up_scale[0])])
    (tokens,) = after((tokens,), (both,))
    both = lax.all_gather(both, "x", axis=0, tiled=True)

    chunks = {0: prepare(tokens, norm_gain, route_ids, route_weights)}
    for step in (1, 2, 3):
        chunks[-step] = [shift(a, "z", NZ, 1) for a in chunks[1 - step]]
        chunks[step] = [shift(a, "z", NZ, -1) for a in chunks[step - 1]]
    chunks[4] = [shift(chunks[-3][0], "z", NZ, 1), shift(chunks[3][1], "z", NZ, -1)]

    down_own = scaled([(down_q[0], down_scale[0])])
    (down_own,) = after((down_own,), chunks[DOWN_AFTER])
    low, high = shift(down_own, "x", NX, 1), shift(down_own, "x", NX, -1)
    far = [
        shift(low[: units // 2], "x", NX, 1),
        shift(high[units // 2 :], "x", NX, -1),
    ]

    stride = CAP * NZ
    hidden, start, at_mix = [], 0, {}
    for group in GROUPS:
        rows = -(-CAP * sum(len(stage) for stage in group) // 8) * 8
        blocks, used = None, 0
        for stage in group:
            arrays, places = [], []
            for j in stage:
                arrays += chunks[j]
                places += [float(used)] * 2
                at_mix[j] = float(start + used)
                used += CAP
            blocks = dispatch(z_at, arrays, places, rows, blocks)
        rows_in = exchange(blocks.reshape(plane, rows, width)).reshape(plane * rows, width)
        units_out = hidden_units(rows_in, both)
        hidden.append(units_out.reshape(plane, rows, units)[:, :used])
        start += used
    hidden = jnp.concatenate(hidden, axis=1).reshape(plane * stride, units)

    order = (4, 3, -3, 2, -2, 1, -1, 0)
    mix = mixing(
        z_at, [a for j in order for a in chunks[j]], [at_mix[j] for j in order for _ in (0, 1)], stride
    )
    sizes = [half, half] + [tok_rows] * (NZ - 1)

    finals, sums, held, last = [], (), (), ()
    for weights in SLICES:
        weights = [{"own": [down_own], "low": [low], "high": [high], "far": far}[w] for w in weights]
        (out,) = after((project_down(hidden, weights),), sums)
        cols = out.shape[1]
        back = exchange(out.reshape(plane, stride, cols)).reshape(plane * stride, cols)
        (back,) = after((back,), held)
        every = [combine(back, mix, sizes, p, SPLIT) for p in range(SPLIT)]
        sums = [a for part in every for a in part]
        moving = [[shift(s[0], "z", NZ, 1), shift(s[1], "z", NZ, -1)] for s in every]
        for step in (2, 4, 6):
            for p, s in enumerate(every):
                pair = after(moving[p], last) if step == 2 and FORCE else moving[p]
                ahead, behind = join(s[step], s[step + 1], *pair)
                moving[p] = [shift(ahead, "z", NZ, 1), shift(behind, "z", NZ, -1)]
            if step == HOLD:
                held = [a for pair in moving for a in pair]
        last = [a for pair in moving for a in pair]
        for s, pair in zip(every, moving):
            finals += [s[8], *pair]
    offsets = [{"own": 0, "low": NX - 1, "high": 1, "far": 2}[w] for s in SLICES for w in s]
    each = len(offsets) // (SPLIT * len(SLICES))
    return finish(x_at, finals, [offsets[i : i + each] for i in range(0, len(offsets), each)])


def solution(mesh):
    assert mesh.devices.shape == (NZ * NY * NC, NX)
    fine = Mesh(mesh.devices.reshape(NZ, NY, NC, NX), ("z", "y", "core", "x"))
    expert = ("z", "y", "core")
    every = ("z", "y", "core", "x")
    in_specs = (
        P(every, None),
        P(),
        P(every, None),
        P(every, None),
        P(expert, "x", None),
        P(expert, "x", None),
        P(expert, "x", None),
        P(expert, "x", None),
        P(expert, None, "x"),
        P(expert, None, "x"),
    )
    return jax.shard_map(
        body, mesh=fine, in_specs=in_specs, out_specs=P(every, None), check_vma=False
    )
```

```python
import functools

import jax
import jax.numpy as jnp
from jax import lax
from jax.experimental import pallas as pl
from jax.experimental.pallas import tpu as pltpu
from jax.sharding import Mesh
from jax.sharding import PartitionSpec as P

BF = jnp.bfloat16
F32 = jnp.float32
VMEM_LIMIT = 52 * 1024 * 1024
CAP = 10
TOK, TOP = 128, 4
LANES = 128
SLICES = (
    (("own", 0), ("own", 1), ("low", 0), ("high", 0)),
    (("low", 1), ("high", 1), ("far", 0), ("far", 1)),
)
SPLIT = 2
FORCE = True
HOLD = 2
DOWN_AFTER = 2
NZ, NY, NC, NX = 8, 4, 2, 4
GROUPS = (((0, -1, 1), (-2, 2)), ((-3, 3), (4,)))


def params(**kw):
    return pltpu.CompilerParams(vmem_limit_bytes=VMEM_LIMIT, **kw)


def shift(array, axis, size, by):
    return lax.ppermute(array, axis, [(i, (i + by) % size) for i in range(size)])


def exchange(blocks):
    return lax.all_to_all(blocks, ("y", "core"), split_axis=0, concat_axis=0, tiled=True)


def after(arrays, earlier):
    return lax.optimization_barrier((tuple(arrays), tuple(earlier)))[0]


def prepare_kernel(tok_ref, gain_ref, ids_ref, weights_ref, *outs):
    rows, width = tok_ref.shape
    half = rows // 2
    top = ids_ref.shape[1]
    experts = lax.broadcasted_iota(jnp.int32, (rows, LANES), 1)
    chosen = [(ids_ref[:, k : k + 1] == experts).astype(F32) for k in range(top)]
    counts = sum(chosen).astype(BF)
    earlier = (
        lax.broadcasted_iota(jnp.int32, (rows, rows), 0)
        > lax.broadcasted_iota(jnp.int32, (rows, rows), 1)
    )
    before = jnp.dot(earlier.astype(F32).astype(BF), counts, preferred_element_type=F32)
    lane = lax.broadcasted_iota(jnp.int32, (rows, LANES), 1)
    routes = jnp.zeros((rows, LANES), F32)
    for k in range(top):
        rank = jnp.sum(chosen[k] * before, axis=1, keepdims=True)
        routes = jnp.where(lane == k, ids_ref[:, k : k + 1].astype(F32), routes)
        routes = jnp.where(lane == top + k, rank, routes)
        routes = jnp.where(lane == 2 * top + k, weights_ref[:, k : k + 1].astype(F32), routes)
    routes = routes.astype(BF)
    for n, out_ref in enumerate(outs):
        values = tok_ref[n * half : (n + 1) * half, :].astype(F32)
        mean_square = jnp.mean(values * values, axis=-1, keepdims=True)
        out_ref[:, :width] = (
            values * lax.rsqrt(mean_square + 1e-06) * gain_ref[...].astype(F32)
        ).astype(BF)
        out_ref[:, width:] = routes[n * half : (n + 1) * half]


def prepare(tokens, gain, ids, weights):
    rows, width = tokens.shape
    half = jax.ShapeDtypeStruct((rows // 2, width + LANES), BF)
    return pl.pallas_call(
        prepare_kernel,
        out_shape=[half, half],
        compiler_params=params(),
        name="prepare",
    )(tokens, gain.reshape(1, width), ids, weights)


def scale_kernel(first, *refs):
    count = (len(refs) - 1) // 2
    scales, values, out_ref = refs[:count], refs[count : 2 * count], refs[-1]
    rows = values[0].shape[0]
    at = 0
    for scale_ref, q_ref in zip(scales, values):
        for c in range(q_ref.shape[1] // 128):
            for r in range(rows // 128):
                block = pl.program_id(0) * (rows // 128) + r
                out_ref[r * 128 : (r + 1) * 128, at : at + 128] = (
                    q_ref[r * 128 : (r + 1) * 128, c * 128 : (c + 1) * 128].astype(F32)
                    * scale_ref[block, first + c]
                ).astype(BF)
            at += 128


def scaled(pairs, part=0, parts=1):
    rows, cols = pairs[0][0].shape
    cols = cols // parts
    tile = 256
    blocks = cols // 128
    return pl.pallas_call(
        functools.partial(scale_kernel, part * blocks),
        grid=(rows // tile,),
        in_specs=[pl.BlockSpec(memory_space=pltpu.SMEM)] * len(pairs)
        + [pl.BlockSpec((tile, cols), lambda i: (i, part))] * len(pairs),
        out_specs=pl.BlockSpec((tile, cols * len(pairs)), lambda i: (i, 0)),
        out_shape=jax.ShapeDtypeStruct((rows, cols * len(pairs)), BF),
        compiler_params=params(),
        name="scaled",
    )(*[s.astype(F32) for _, s in pairs], *[q for q, _ in pairs])


def slots_of(info, low, stride, at, k):
    local = info[:, k : k + 1] - low
    here = (local >= 0.0) & (local < float(NY * NC))
    return jnp.where(here, local * float(stride) + info[:, TOP + k : TOP + k + 1] + at, -1.0)


def dispatch_kernel(places, rows, based, z_at, *refs):
    count = len(places)
    chunks, routes = refs[:count], refs[count : 2 * count]
    out_ref, pick_ref, chunk_ref = refs[-3:]
    half = chunks[0].shape[0]

    @pl.when(pl.program_id(0) == 0)
    def _():
        low = (z_at[0] * (NY * NC)).astype(F32)
        for n, at in enumerate(places):
            info = routes[n][...].astype(F32)
            slots = lax.broadcasted_iota(jnp.int32, (half, pick_ref.shape[0]), 1).astype(F32)
            pick = jnp.zeros(slots.shape, F32)
            for k in range(TOP):
                pick = jnp.where(slots_of(info, low, rows, at, k) == slots, 1.0, pick)
            if n % 2:
                both = jnp.concatenate([other, pick], axis=0)
                pick_ref[:, (n - 1) * half : (n + 1) * half] = both.T.astype(BF)
            other = pick

    for n, ref in enumerate(chunks):
        chunk_ref[n * half : (n + 1) * half, :] = ref[...]
    total = jnp.dot(pick_ref[...], chunk_ref[...], preferred_element_type=F32)
    if based:
        total = total + refs[2 * count][...].astype(F32)
    out_ref[...] = total.astype(BF)


def dispatch(z_at, chunks, places, rows, base):
    plane = NY * NC
    half = chunks[0].shape[0]
    width = chunks[0].shape[1] - LANES
    tile = min(1024, width)
    bases = [] if base is None else [base]
    out_spec = pl.BlockSpec((plane * rows, tile), lambda i, z: (0, i))
    return pl.pallas_call(
        functools.partial(dispatch_kernel, places, rows, bool(bases)),
        grid_spec=pltpu.PrefetchScalarGridSpec(
            num_scalar_prefetch=1,
            grid=(width // tile,),
            in_specs=[pl.BlockSpec((half, tile), lambda i, z: (0, i))] * len(chunks)
            + [pl.BlockSpec((half, LANES), lambda i, z: (0, width // LANES))] * len(chunks)
            + [out_spec] * len(bases),
            out_specs=out_spec,
            scratch_shapes=[
                pltpu.VMEM((plane * rows, len(chunks) * half), BF),
                pltpu.VMEM((len(chunks) * half, tile), BF),
            ],
        ),
        out_shape=jax.ShapeDtypeStruct((plane * rows, width), BF),
        compiler_params=params(),
        name="dispatch",
    )(z_at, *chunks, *chunks, *bases)


def mixing_kernel(places, stride, z_at, *refs):
    routes, out_ref = refs[:-1], refs[-1]
    half = routes[0].shape[0]
    low = (z_at[0] * (NY * NC)).astype(F32)
    for n, at in enumerate(places):
        info = routes[n][...].astype(F32)
        slots = lax.broadcasted_iota(jnp.int32, (half, out_ref.shape[1]), 1).astype(F32)
        mix = jnp.zeros(slots.shape, F32)
        for k in range(TOP):
            weight = info[:, 2 * TOP + k : 2 * TOP + k + 1]
            mix = jnp.where(slots_of(info, low, stride, at, k) == slots, weight, mix)
        out_ref[n * half : (n + 1) * half, :] = mix.astype(BF)


def mixing(z_at, chunks, places, stride):
    half, width = chunks[0].shape
    return pl.pallas_call(
        functools.partial(mixing_kernel, places, stride),
        grid_spec=pltpu.PrefetchScalarGridSpec(
            num_scalar_prefetch=1,
            grid=(1,),
            in_specs=[pl.BlockSpec((half, LANES), lambda i, z: (0, width // LANES - 1))]
            * len(chunks),
            out_specs=pl.BlockSpec((len(chunks) * half, NY * NC * stride), lambda i, z: (0, 0)),
        ),
        out_shape=jax.ShapeDtypeStruct((len(chunks) * half, NY * NC * stride), BF),
        compiler_params=params(),
        name="mixing",
    )(z_at, *chunks)


def hidden_kernel(rows_ref, gate_ref, up_ref, out_ref):
    gate = jnp.dot(rows_ref[...], gate_ref[...], preferred_element_type=F32)
    up = jnp.dot(rows_ref[...], up_ref[...], preferred_element_type=F32)
    out_ref[...] = (gate / (1.0 + jnp.exp(-gate)) * up).astype(BF)


def hidden_units(rows, both):
    count, width = rows.shape
    units = both.shape[1] // 2
    tile = 256
    steps = units // tile
    return pl.pallas_call(
        hidden_kernel,
        grid=(steps,),
        in_specs=[
            pl.BlockSpec((count, width), lambda i: (0, 0)),
            pl.BlockSpec((width, tile), lambda i: (0, i)),
            pl.BlockSpec((width, tile), lambda i: (0, i + steps)),
        ],
        out_specs=pl.BlockSpec((count, tile), lambda i: (0, i)),
        out_shape=jax.ShapeDtypeStruct((count, units), BF),
        compiler_params=params(),
        name="hidden_units",
    )(rows, both, both)


def down_kernel(counts, hidden_ref, *refs):
    weights, out_ref = list(refs[:-1]), refs[-1]
    left = 0
    for count in counts:
        pieces, weights = weights[:count], weights[count:]
        width = pieces[0].shape[1]
        tile = min(512, width)
        for t in range(width // tile):
            at, total = 0, None
            for ref in pieces:
                part = jnp.dot(
                    hidden_ref[:, at : at + ref.shape[0]],
                    ref[:, t * tile : (t + 1) * tile],
                    preferred_element_type=F32,
                )
                total = part if total is None else total + part
                at += ref.shape[0]
            out_ref[:, left : left + tile] = total.astype(BF)
            left += tile


def project_down(hidden, slices):
    width = sum(s[0].shape[1] for s in slices)
    return pl.pallas_call(
        functools.partial(down_kernel, [len(s) for s in slices]),
        out_shape=jax.ShapeDtypeStruct((hidden.shape[0], width), BF),
        compiler_params=params(),
        name="project_down",
    )(hidden, *[w for s in slices for w in s])


def combine_kernel(rows_ref, mix_ref, *outs):
    at = 0
    for out_ref in outs:
        out_ref[...] = jnp.dot(
            mix_ref[at : at + out_ref.shape[0], :], rows_ref[...], preferred_element_type=F32
        ).astype(BF)
        at += out_ref.shape[0]


def combine(rows, mix, sizes, part, parts):
    count, width = rows.shape[0], rows.shape[1] // parts
    tile = min(512, width)
    first = part * (width // tile)
    return pl.pallas_call(
        combine_kernel,
        grid=(width // tile,),
        in_specs=[
            pl.BlockSpec((count, tile), lambda i: (0, i + first)),
            pl.BlockSpec(mix.shape, lambda i: (0, 0)),
        ],
        out_specs=[pl.BlockSpec((m, tile), lambda i: (0, i)) for m in sizes],
        out_shape=[jax.ShapeDtypeStruct((m, width), BF) for m in sizes],
        compiler_params=params(),
        name="combine",
    )(rows, mix)


def join_kernel(ahead_ref, behind_ref, up_ref, down_ref, ahead_out, behind_out):
    size, half = ahead_ref.shape[0], up_ref.shape[0]
    for here, came, at, out in (
        (ahead_ref, up_ref, 0, ahead_out),
        (behind_ref, down_ref, size - half, behind_out),
    ):
        if half < size:
            out[...] = here[...]
        out[at : at + half, :] = (
            here[at : at + half, :].astype(F32) + came[...].astype(F32)
        ).astype(BF)


def join(ahead, behind, up, down):
    return pl.pallas_call(
        join_kernel,
        out_shape=[jax.ShapeDtypeStruct(ahead.shape, BF)] * 2,
        compiler_params=params(),
        name="join",
    )(ahead, behind, up, down)


def finish_kernel(offsets, x_at, *refs):
    parts, out_ref = refs[:-1], refs[-1]
    width = out_ref.shape[1] // (2 * NX)
    own = x_at[0]
    for n, slices in enumerate(offsets):
        kept, ahead, behind = parts[3 * n : 3 * n + 3]
        for i, (offset, side) in enumerate(slices):
            cols = slice(i * width, (i + 1) * width)
            total = (
                kept[:, cols].astype(F32) + ahead[:, cols].astype(F32) + behind[:, cols].astype(F32)
            )
            place = pl.multiple_of((lax.rem(own + offset, NX) * 2 + side) * width, 128)
            out_ref[:, pl.ds(place, width)] = total.astype(BF)


def finish(x_at, parts, offsets):
    rows = parts[0].shape[0]
    width = sum(p.shape[1] for p in parts[::3])
    return pl.pallas_call(
        functools.partial(finish_kernel, offsets),
        grid_spec=pltpu.PrefetchScalarGridSpec(
            num_scalar_prefetch=1,
            grid=(1,),
            in_specs=[pl.BlockSpec(p.shape, lambda i, s: (0, 0)) for p in parts],
            out_specs=pl.BlockSpec((rows, width), lambda i, s: (0, 0)),
        ),
        out_shape=jax.ShapeDtypeStruct((rows, width), BF),
        compiler_params=params(),
        name="finish",
    )(x_at, *parts)


def body(
    tokens,
    norm_gain,
    route_ids,
    route_weights,
    gate_q,
    gate_scale,
    up_q,
    up_scale,
    down_q,
    down_scale,
):
    tok_rows, width = tokens.shape
    units = down_q.shape[1]
    assert tok_rows == TOK and route_ids.shape[1] == TOP
    half = tok_rows // 2
    plane = NY * NC
    z_at = jnp.reshape(lax.axis_index("z"), (1,)).astype(jnp.int32)
    x_at = jnp.reshape(lax.axis_index("x"), (1,)).astype(jnp.int32)

    both = scaled([(gate_q[0], gate_scale[0]), (up_q[0], up_scale[0])])
    (tokens,) = after((tokens,), (both,))
    both = lax.all_gather(both, "x", axis=0, tiled=True)

    chunks = {0: prepare(tokens, norm_gain, route_ids, route_weights)}
    for step in (1, 2, 3):
        chunks[-step] = [shift(a, "z", NZ, 1) for a in chunks[1 - step]]
        chunks[step] = [shift(a, "z", NZ, -1) for a in chunks[step - 1]]
    chunks[4] = [shift(chunks[-3][0], "z", NZ, 1), shift(chunks[3][1], "z", NZ, -1)]

    pair = [(down_q[0], down_scale[0])]
    downs = {}
    for part in range(2):
        (own,) = after((scaled(pair, part, 2),), chunks[DOWN_AFTER])
        low, high = shift(own, "x", NX, 1), shift(own, "x", NX, -1)
        downs["own", part], downs["low", part], downs["high", part] = [own], [low], [high]
    for part in range(2):
        (low,), (high,) = downs["low", part], downs["high", part]
        downs["far", part] = [
            shift(low[: units // 2], "x", NX, 1),
            shift(high[units // 2 :], "x", NX, -1),
        ]

    stride = CAP * NZ
    order = (4, 3, -3, 2, -2, 1, -1, 0)
    placed = [j for group in GROUPS for stage in group for j in stage]
    places = [float(CAP * placed.index(j)) for j in order for _ in range(2)]
    mix = mixing(z_at, [a for j in order for a in chunks[j]], places, stride)
    hidden = []
    for group in GROUPS:
        rows = -(-CAP * sum(len(stage) for stage in group) // 8) * 8
        blocks, used = None, 0
        for stage in group:
            arrays, places = [], []
            for j in stage:
                arrays += chunks[j]
                places += [float(used)] * 2
                used += CAP
            blocks = dispatch(z_at, arrays, places, rows, blocks)
        rows_in = exchange(blocks.reshape(plane, rows, width)).reshape(plane * rows, width)
        if not hidden:
            (rows_in,) = after((rows_in,), (mix,))
        units_out = hidden_units(rows_in, both)
        hidden.append(units_out.reshape(plane, rows, units)[:, :used])
    hidden = jnp.concatenate(hidden, axis=1).reshape(plane * stride, units)

    sizes = [half, half] + [tok_rows] * (NZ - 1)

    finals, came, held, last = [], (), (), ()
    for weights in SLICES:
        (out,) = after((project_down(hidden, [downs[w] for w in weights]),), came)
        cols = out.shape[1]
        back = exchange(out.reshape(plane, stride, cols)).reshape(plane * stride, cols)
        came = (back,)
        (back,) = after((back,), held)
        every = [combine(back, mix, sizes, p, SPLIT) for p in range(SPLIT)]
        moving = [[shift(s[0], "z", NZ, 1), shift(s[1], "z", NZ, -1)] for s in every]
        for step in (2, 4, 6):
            for p, s in enumerate(every):
                pair = after(moving[p], last) if step == 2 and FORCE else moving[p]
                ahead, behind = join(s[step], s[step + 1], *pair)
                moving[p] = [shift(ahead, "z", NZ, 1), shift(behind, "z", NZ, -1)]
            if step == HOLD:
                held = [a for pair in moving for a in pair]
        last = [a for pair in moving for a in pair]
        for s, pair in zip(every, moving):
            finals += [s[8], *pair]
    away = {"own": 0, "low": NX - 1, "high": 1, "far": 2}
    offsets = [(away[w], part) for s in SLICES for w, part in s]
    each = len(offsets) // (SPLIT * len(SLICES))
    return finish(x_at, finals, [offsets[i : i + each] for i in range(0, len(offsets), each)])


def solution(mesh):
    assert mesh.devices.shape == (NZ * NY * NC, NX)
    fine = Mesh(mesh.devices.reshape(NZ, NY, NC, NX), ("z", "y", "core", "x"))
    expert = ("z", "y", "core")
    every = ("z", "y", "core", "x")
    in_specs = (
        P(every, None),
        P(),
        P(every, None),
        P(every, None),
        P(expert, "x", None),
        P(expert, "x", None),
        P(expert, "x", None),
        P(expert, "x", None),
        P(expert, None, "x"),
        P(expert, None, "x"),
    )
    return jax.shard_map(
        body, mesh=fine, in_specs=in_specs, out_specs=P(every, None), check_vma=False
    )
```

```python
import functools

import jax
import jax.numpy as jnp
from jax import lax
from jax.experimental import pallas as pl
from jax.experimental.pallas import tpu as pltpu
from jax.sharding import Mesh
from jax.sharding import PartitionSpec as P

BF = jnp.bfloat16
F32 = jnp.float32
VMEM_LIMIT = 52 * 1024 * 1024
CAP = 10
TOK, TOP = 128, 4
LANES = 128
SLICES = (
    (("own", 0), ("own", 1), ("low", 0), ("high", 0)),
    (("low", 1), ("high", 1), ("far", 0), ("far", 1)),
)
SPLIT = 2
FORCE = True
HOLD = 2
DOWN_AFTER = 2
NZ, NY, NC, NX = 8, 4, 2, 4
GROUPS = (((0, -1, 1), (-2, 2)), ((-3, 3), (4,)))


def params(**kw):
    return pltpu.CompilerParams(vmem_limit_bytes=VMEM_LIMIT, **kw)


def shift(array, axis, size, by):
    return lax.ppermute(array, axis, [(i, (i + by) % size) for i in range(size)])


def exchange(blocks):
    return lax.all_to_all(blocks, ("y", "core"), split_axis=0, concat_axis=0, tiled=True)


def after(arrays, earlier):
    return lax.optimization_barrier((tuple(arrays), tuple(earlier)))[0]


def prepare_kernel(tok_ref, gain_ref, ids_ref, weights_ref, *outs):
    rows, width = tok_ref.shape
    half = rows // 2
    top = ids_ref.shape[1]
    experts = lax.broadcasted_iota(jnp.int32, (rows, LANES), 1)
    chosen = [(ids_ref[:, k : k + 1] == experts).astype(F32) for k in range(top)]
    counts = sum(chosen).astype(BF)
    earlier = (
        lax.broadcasted_iota(jnp.int32, (rows, rows), 0)
        > lax.broadcasted_iota(jnp.int32, (rows, rows), 1)
    )
    before = jnp.dot(earlier.astype(F32).astype(BF), counts, preferred_element_type=F32)
    lane = lax.broadcasted_iota(jnp.int32, (rows, LANES), 1)
    routes = jnp.zeros((rows, LANES), F32)
    for k in range(top):
        rank = jnp.sum(chosen[k] * before, axis=1, keepdims=True)
        routes = jnp.where(lane == k, ids_ref[:, k : k + 1].astype(F32), routes)
        routes = jnp.where(lane == top + k, rank, routes)
        routes = jnp.where(lane == 2 * top + k, weights_ref[:, k : k + 1].astype(F32), routes)
    routes = routes.astype(BF)
    for n, out_ref in enumerate(outs):
        values = tok_ref[n * half : (n + 1) * half, :].astype(F32)
        mean_square = jnp.mean(values * values, axis=-1, keepdims=True)
        out_ref[:, :width] = (
            values * lax.rsqrt(mean_square + 1e-06) * gain_ref[...].astype(F32)
        ).astype(BF)
        out_ref[:, width:] = routes[n * half : (n + 1) * half]


def prepare(tokens, gain, ids, weights):
    rows, width = tokens.shape
    half = jax.ShapeDtypeStruct((rows // 2, width + LANES), BF)
    return pl.pallas_call(
        prepare_kernel,
        out_shape=[half, half],
        compiler_params=params(),
        name="prepare",
    )(tokens, gain.reshape(1, width), ids, weights)


def scale_kernel(first, *refs):
    count = (len(refs) - 1) // 2
    scales, values, out_ref = refs[:count], refs[count : 2 * count], refs[-1]
    rows = values[0].shape[0]
    at = 0
    for scale_ref, q_ref in zip(scales, values):
        for c in range(q_ref.shape[1] // 128):
            for r in range(rows // 128):
                block = pl.program_id(0) * (rows // 128) + r
                out_ref[r * 128 : (r + 1) * 128, at : at + 128] = (
                    q_ref[r * 128 : (r + 1) * 128, c * 128 : (c + 1) * 128].astype(F32)
                    * scale_ref[block, first + c]
                ).astype(BF)
            at += 128


def scaled(pairs, part=0, parts=1):
    rows, cols = pairs[0][0].shape
    cols = cols // parts
    tile = 256
    blocks = cols // 128
    return pl.pallas_call(
        functools.partial(scale_kernel, part * blocks),
        grid=(rows // tile,),
        in_specs=[pl.BlockSpec(memory_space=pltpu.SMEM)] * len(pairs)
        + [pl.BlockSpec((tile, cols), lambda i: (i, part))] * len(pairs),
        out_specs=pl.BlockSpec((tile, cols * len(pairs)), lambda i: (i, 0)),
        out_shape=jax.ShapeDtypeStruct((rows, cols * len(pairs)), BF),
        compiler_params=params(),
        name="scaled",
    )(*[s.astype(F32) for _, s in pairs], *[q for q, _ in pairs])


def slots_of(info, low, stride, at, k):
    local = info[:, k : k + 1] - low
    here = (local >= 0.0) & (local < float(NY * NC))
    return jnp.where(here, local * float(stride) + info[:, TOP + k : TOP + k + 1] + at, -1.0)


def dispatch_kernel(places, rows, based, z_at, *refs):
    count = len(places)
    chunks, routes = refs[:count], refs[count : 2 * count]
    out_ref, pick_ref, chunk_ref = refs[-3:]
    half = chunks[0].shape[0]

    @pl.when(pl.program_id(0) == 0)
    def _():
        low = (z_at[0] * (NY * NC)).astype(F32)
        for n, at in enumerate(places):
            info = routes[n][...].astype(F32)
            slots = lax.broadcasted_iota(jnp.int32, (half, pick_ref.shape[0]), 1).astype(F32)
            pick = jnp.zeros(slots.shape, F32)
            for k in range(TOP):
                pick = jnp.where(slots_of(info, low, rows, at, k) == slots, 1.0, pick)
            if n % 2:
                both = jnp.concatenate([other, pick], axis=0)
                pick_ref[:, (n - 1) * half : (n + 1) * half] = both.T.astype(BF)
            other = pick

    for n, ref in enumerate(chunks):
        chunk_ref[n * half : (n + 1) * half, :] = ref[...]
    total = jnp.dot(pick_ref[...], chunk_ref[...], preferred_element_type=F32)
    if based:
        total = total + refs[2 * count][...].astype(F32)
    out_ref[...] = total.astype(BF)


def dispatch(z_at, chunks, places, rows, base):
    plane = NY * NC
    half = chunks[0].shape[0]
    width = chunks[0].shape[1] - LANES
    tile = min(1024, width)
    bases = [] if base is None else [base]
    out_spec = pl.BlockSpec((plane * rows, tile), lambda i, z: (0, i))
    return pl.pallas_call(
        functools.partial(dispatch_kernel, places, rows, bool(bases)),
        grid_spec=pltpu.PrefetchScalarGridSpec(
            num_scalar_prefetch=1,
            grid=(width // tile,),
            in_specs=[pl.BlockSpec((half, tile), lambda i, z: (0, i))] * len(chunks)
            + [pl.BlockSpec((half, LANES), lambda i, z: (0, width // LANES))] * len(chunks)
            + [out_spec] * len(bases),
            out_specs=out_spec,
            scratch_shapes=[
                pltpu.VMEM((plane * rows, len(chunks) * half), BF),
                pltpu.VMEM((len(chunks) * half, tile), BF),
            ],
        ),
        out_shape=jax.ShapeDtypeStruct((plane * rows, width), BF),
        compiler_params=params(),
        name="dispatch",
    )(z_at, *chunks, *chunks, *bases)


def mixing_kernel(places, stride, z_at, *refs):
    routes, out_ref = refs[:-1], refs[-1]
    half = routes[0].shape[0]
    low = (z_at[0] * (NY * NC)).astype(F32)
    for n, at in enumerate(places):
        info = routes[n][...].astype(F32)
        slots = lax.broadcasted_iota(jnp.int32, (half, out_ref.shape[1]), 1).astype(F32)
        mix = jnp.zeros(slots.shape, F32)
        for k in range(TOP):
            weight = info[:, 2 * TOP + k : 2 * TOP + k + 1]
            mix = jnp.where(slots_of(info, low, stride, at, k) == slots, weight, mix)
        out_ref[n * half : (n + 1) * half, :] = mix.astype(BF)


def mixing(z_at, chunks, places, stride):
    half, width = chunks[0].shape
    return pl.pallas_call(
        functools.partial(mixing_kernel, places, stride),
        grid_spec=pltpu.PrefetchScalarGridSpec(
            num_scalar_prefetch=1,
            grid=(1,),
            in_specs=[pl.BlockSpec((half, LANES), lambda i, z: (0, width // LANES - 1))]
            * len(chunks),
            out_specs=pl.BlockSpec((len(chunks) * half, NY * NC * stride), lambda i, z: (0, 0)),
        ),
        out_shape=jax.ShapeDtypeStruct((len(chunks) * half, NY * NC * stride), BF),
        compiler_params=params(),
        name="mixing",
    )(z_at, *chunks)


def hidden_kernel(rows_ref, gate_ref, up_ref, out_ref):
    gate = jnp.dot(rows_ref[...], gate_ref[...], preferred_element_type=F32)
    up = jnp.dot(rows_ref[...], up_ref[...], preferred_element_type=F32)
    out_ref[...] = (gate / (1.0 + jnp.exp(-gate)) * up).astype(BF)


def hidden_units(rows, both):
    count, width = rows.shape
    units = both.shape[1] // 2
    tile = 256
    steps = units // tile
    return pl.pallas_call(
        hidden_kernel,
        grid=(steps,),
        in_specs=[
            pl.BlockSpec((count, width), lambda i: (0, 0)),
            pl.BlockSpec((width, tile), lambda i: (0, i)),
            pl.BlockSpec((width, tile), lambda i: (0, i + steps)),
        ],
        out_specs=pl.BlockSpec((count, tile), lambda i: (0, i)),
        out_shape=jax.ShapeDtypeStruct((count, units), BF),
        compiler_params=params(),
        name="hidden_units",
    )(rows, both, both)


def down_kernel(counts, hidden_ref, *refs):
    weights, out_ref = list(refs[:-1]), refs[-1]
    left = 0
    for count in counts:
        pieces, weights = weights[:count], weights[count:]
        width = pieces[0].shape[1]
        tile = min(512, width)
        for t in range(width // tile):
            at, total = 0, None
            for ref in pieces:
                part = jnp.dot(
                    hidden_ref[:, at : at + ref.shape[0]],
                    ref[:, t * tile : (t + 1) * tile],
                    preferred_element_type=F32,
                )
                total = part if total is None else total + part
                at += ref.shape[0]
            out_ref[:, left : left + tile] = total.astype(BF)
            left += tile


def project_down(hidden, slices):
    width = sum(s[0].shape[1] for s in slices)
    return pl.pallas_call(
        functools.partial(down_kernel, [len(s) for s in slices]),
        out_shape=jax.ShapeDtypeStruct((hidden.shape[0], width), BF),
        compiler_params=params(),
        name="project_down",
    )(hidden, *[w for s in slices for w in s])


def combine_kernel(rows_ref, mix_ref, *outs):
    at = 0
    for out_ref in outs:
        out_ref[...] = jnp.dot(
            mix_ref[at : at + out_ref.shape[0], :], rows_ref[...], preferred_element_type=F32
        ).astype(BF)
        at += out_ref.shape[0]


def combine(rows, mix, sizes, part, parts):
    count, width = rows.shape[0], rows.shape[1] // parts
    tile = min(512, width)
    first = part * (width // tile)
    return pl.pallas_call(
        combine_kernel,
        grid=(width // tile,),
        in_specs=[
            pl.BlockSpec((count, tile), lambda i: (0, i + first)),
            pl.BlockSpec(mix.shape, lambda i: (0, 0)),
        ],
        out_specs=[pl.BlockSpec((m, tile), lambda i: (0, i)) for m in sizes],
        out_shape=[jax.ShapeDtypeStruct((m, width), BF) for m in sizes],
        compiler_params=params(),
        name="combine",
    )(rows, mix)


def join_kernel(ahead_ref, behind_ref, up_ref, down_ref, ahead_out, behind_out):
    size, half = ahead_ref.shape[0], up_ref.shape[0]
    for here, came, at, out in (
        (ahead_ref, up_ref, 0, ahead_out),
        (behind_ref, down_ref, size - half, behind_out),
    ):
        if half < size:
            out[...] = here[...]
        out[at : at + half, :] = (
            here[at : at + half, :].astype(F32) + came[...].astype(F32)
        ).astype(BF)


def join(ahead, behind, up, down):
    return pl.pallas_call(
        join_kernel,
        out_shape=[jax.ShapeDtypeStruct(ahead.shape, BF)] * 2,
        compiler_params=params(),
        name="join",
    )(ahead, behind, up, down)


def finish_kernel(offsets, x_at, *refs):
    parts, out_ref = refs[:-1], refs[-1]
    width = out_ref.shape[1] // (2 * NX)
    own = x_at[0]
    for n, slices in enumerate(offsets):
        kept, ahead, behind = parts[3 * n : 3 * n + 3]
        for i, (offset, side) in enumerate(slices):
            cols = slice(i * width, (i + 1) * width)
            total = (
                kept[:, cols].astype(F32) + ahead[:, cols].astype(F32) + behind[:, cols].astype(F32)
            )
            place = pl.multiple_of((lax.rem(own + offset, NX) * 2 + side) * width, 128)
            out_ref[:, pl.ds(place, width)] = total.astype(BF)


def finish(x_at, parts, offsets):
    rows = parts[0].shape[0]
    width = sum(p.shape[1] for p in parts[::3])
    return pl.pallas_call(
        functools.partial(finish_kernel, offsets),
        grid_spec=pltpu.PrefetchScalarGridSpec(
            num_scalar_prefetch=1,
            grid=(1,),
            in_specs=[pl.BlockSpec(p.shape, lambda i, s: (0, 0)) for p in parts],
            out_specs=pl.BlockSpec((rows, width), lambda i, s: (0, 0)),
        ),
        out_shape=jax.ShapeDtypeStruct((rows, width), BF),
        compiler_params=params(),
        name="finish",
    )(x_at, *parts)


def body(
    tokens,
    norm_gain,
    route_ids,
    route_weights,
    gate_q,
    gate_scale,
    up_q,
    up_scale,
    down_q,
    down_scale,
):
    tok_rows, width = tokens.shape
    units = down_q.shape[1]
    assert tok_rows == TOK and route_ids.shape[1] == TOP
    half = tok_rows // 2
    plane = NY * NC
    z_at = jnp.reshape(lax.axis_index("z"), (1,)).astype(jnp.int32)
    x_at = jnp.reshape(lax.axis_index("x"), (1,)).astype(jnp.int32)

    both = scaled([(gate_q[0], gate_scale[0]), (up_q[0], up_scale[0])])
    (tokens,) = after((tokens,), (both,))
    both = lax.all_gather(both, "x", axis=0, tiled=True)

    chunks = {0: prepare(tokens, norm_gain, route_ids, route_weights)}
    for step in (1, 2, 3):
        chunks[-step] = [shift(a, "z", NZ, 1) for a in chunks[1 - step]]
        chunks[step] = [shift(a, "z", NZ, -1) for a in chunks[step - 1]]
    chunks[4] = [shift(chunks[-3][0], "z", NZ, 1), shift(chunks[3][1], "z", NZ, -1)]

    pair = [(down_q[0], down_scale[0])]
    downs = {}
    for part in range(2):
        (own,) = after((scaled(pair, part, 2),), chunks[DOWN_AFTER])
        low, high = shift(own, "x", NX, 1), shift(own, "x", NX, -1)
        downs["own", part], downs["low", part], downs["high", part] = [own], [low], [high]
    for part in range(2):
        (low,), (high,) = downs["low", part], downs["high", part]
        downs["far", part] = [
            shift(low[: units // 2], "x", NX, 1),
            shift(high[units // 2 :], "x", NX, -1),
        ]

    stride = CAP * NZ
    order = (4, 3, -3, 2, -2, 1, -1, 0)
    placed = [j for group in GROUPS for stage in group for j in stage]
    places = [float(CAP * placed.index(j)) for j in order for _ in range(2)]
    mix = mixing(z_at, [a for j in order for a in chunks[j]], places, stride)
    hidden = []
    for group in GROUPS:
        rows = -(-CAP * sum(len(stage) for stage in group) // 8) * 8
        blocks, used = None, 0
        for stage in group:
            arrays, places = [], []
            for j in stage:
                arrays += chunks[j]
                places += [float(used)] * 2
                used += CAP
            blocks = dispatch(z_at, arrays, places, rows, blocks)
        rows_in = exchange(blocks.reshape(plane, rows, width)).reshape(plane * rows, width)
        if not hidden:
            (rows_in,) = after((rows_in,), (mix,))
        units_out = hidden_units(rows_in, both)
        hidden.append(units_out.reshape(plane, rows, units)[:, :used])
    hidden = jnp.concatenate(hidden, axis=1).reshape(plane * stride, units)
    (hidden,) = after((hidden,), downs["low", 1] + downs["high", 1])

    sizes = [half, half] + [tok_rows] * (NZ - 1)

    finals, came, held, last = [], (), (), ()
    for weights in SLICES:
        (out,) = after((project_down(hidden, [downs[w] for w in weights]),), came)
        cols = out.shape[1]
        back = exchange(out.reshape(plane, stride, cols)).reshape(plane * stride, cols)
        came = (back,)
        (back,) = after((back,), held)
        every = [combine(back, mix, sizes, p, SPLIT) for p in range(SPLIT)]
        moving = [[shift(s[0], "z", NZ, 1), shift(s[1], "z", NZ, -1)] for s in every]
        for step in (2, 4, 6):
            for p, s in enumerate(every):
                pair = after(moving[p], last) if step == 2 and FORCE else moving[p]
                ahead, behind = join(s[step], s[step + 1], *pair)
                moving[p] = [shift(ahead, "z", NZ, 1), shift(behind, "z", NZ, -1)]
            if step == HOLD:
                held = [a for pair in moving for a in pair]
        last = [a for pair in moving for a in pair]
        for s, pair in zip(every, moving):
            finals += [s[8], *pair]
    away = {"own": 0, "low": NX - 1, "high": 1, "far": 2}
    offsets = [(away[w], part) for s in SLICES for w, part in s]
    each = len(offsets) // (SPLIT * len(SLICES))
    return finish(x_at, finals, [offsets[i : i + each] for i in range(0, len(offsets), each)])


def solution(mesh):
    assert mesh.devices.shape == (NZ * NY * NC, NX)
    fine = Mesh(mesh.devices.reshape(NZ, NY, NC, NX), ("z", "y", "core", "x"))
    expert = ("z", "y", "core")
    every = ("z", "y", "core", "x")
    in_specs = (
        P(every, None),
        P(),
        P(every, None),
        P(every, None),
        P(expert, "x", None),
        P(expert, "x", None),
        P(expert, "x", None),
        P(expert, "x", None),
        P(expert, None, "x"),
        P(expert, None, "x"),
    )
    return jax.shard_map(
        body, mesh=fine, in_specs=in_specs, out_specs=P(every, None), check_vma=False
    )
```
